256 devices in a mesh: ep: 128 (over x, z, y), tp: 2 (over core).
Axes of the slice: x: 4, y: 4, z: 8, core: 2. Of those that a mesh axis runs over, the one named last changes fastest.
Arguments:
- query: bfloat16 [128, 32, 8192], P('ep', None, 'tp'), may hold values from -100 to 100
- new_kv: bfloat16 [2, 128, 32, 512], P(None, 'ep', None, 'tp'), may hold values from -4 to 4
- cache: bfloat16 [2, 128, 128, 512], P(None, 'ep', None, 'tp'), may hold values from -4 to 4
- cache_len: int32 [128], P('ep'), may hold values from 2 to 128
- parents: int32 [128, 32], P('ep'), may hold values from 0 to 30, as said below
- hidden: bfloat16 [4096, 4096], P('ep', 'tp'), may hold values from -6 to 6
- moe_gain: float32 [4096], replicated, may hold values from 0.5 to 1.5
- routes: int32 [4096, 8], P('ep'), may hold values from 0 to 127, all different within a row; in each aligned block of 32 rows (0 to 31, 32 to 63, ...) at most 4 rows name the same one
- gates: float32 [4096, 8], P('ep'), may hold values from 0.05 to 1
- w_gate: bfloat16 [128, 4096, 768], P('ep', None, 'tp'), may hold values from -0.09375 to 0.09375
- w_up: bfloat16 [128, 4096, 768], P('ep', None, 'tp'), may hold values from -0.09375 to 0.09375
- w_down: bfloat16 [128, 768, 4096], P('ep', 'tp'), may hold values from -0.21875 to 0.21875
- accept: int32 [128], P('ep'), may hold values from 0 to 31
- final_gain: float32 [4096], replicated, may hold values from 0.5 to 1.5
- medusa_w: bfloat16 [2, 4096, 4096], P(None, ('ep', 'tp')), may hold values from -0.09375 to 0.09375
- medusa_b: float32 [2, 4096], P(None, ('ep', 'tp')), may hold values from -3 to 3
- lm_head: bfloat16 [77824, 4096], P(('ep', 'tp')), may hold values from -12 to 12
Outputs:
- attended: bfloat16 [128, 32, 8192], P('ep', None, 'tp')
- layer_out: bfloat16 [4096, 4096], P('ep', 'tp')
- logprob: float32 [2, 128, 77824], P(None, None, ('ep', 'tp'))
The draws below stay inside these ranges and needn't reach their ends.
Inputs may be any that keep to these rules, and one draw needn't show every extreme that they name: `routes`: each token names 8 different experts; among the tokens of one index of ep no expert is named more than 4 times. `parents`: node 0 is the root and names itself; every other node i names a parent below i.
All inputs are finite; a program needn't handle non-finite values.
Results may differ from the reference program's by a relative error of at most 0.0049.
Values may be sent and summed in bfloat16 or wider, within the bound.
No kernel may reach another device: no remote copies, remote signals or barrier semaphores. Data moves between devices by JAX's collectives and lax.ppermute only.
A program may use at most 128 MiB of HBM per device.

```python
import math
import jax
import jax.numpy as jnp
import numpy as np
from jax import lax

D = 4096
QH = 64
KVH = 4
HD = 128
FF_WIN = 768
TOPK = 8
NODES = 32
MH = 2
REQ_DEV = 1
CACHE = 128
EXPERTS = 128
CAP = 4
VOCAB = 77824
REQUESTS = 128
TOKENS = 4096
N_EP = 128


def cache_base(key):
    return jnp.clip(jax.random.normal(key, (2, REQUESTS, CACHE, KVH * HD), jnp.float32), -4.0, 4.0)


def draw_cache(key, part):
    values = cache_base(key)
    return values.astype(jnp.bfloat16)


def draw_query(key, part):
    key = jax.random.fold_in(key, 7)
    values = jnp.clip(jax.random.normal(key, (REQUESTS, NODES, QH * HD), jnp.float32), -4.0, 4.0)
    return values.astype(jnp.bfloat16)


def draw_cache_len(key, part):
    key = jax.random.fold_in(key, 5)
    lengths = jax.random.randint(key, (REQUESTS,), 2, CACHE + 1)
    chosen = jax.random.randint(jax.random.fold_in(key, 1), (), 0, REQUESTS)
    return jnp.where(jnp.arange(REQUESTS) == chosen, CACHE, lengths).astype(jnp.int32)


def draw_parents(key, part):
    key = jax.random.fold_in(key, 11)
    nodes = jnp.arange(NODES)
    parent = jax.random.randint(key, (REQUESTS, NODES), 0, jnp.maximum(nodes, 1)[None, :])
    chosen = jax.random.randint(jax.random.fold_in(key, 1), (), 0, REQUESTS)
    deepest = (jnp.arange(REQUESTS)[:, None] == chosen) & (nodes[None, :] == NODES - 1)
    return jnp.where(deepest, NODES - 2, parent).astype(jnp.int32)


def draw_lm_head(key, part):
    key = jax.random.fold_in(key, 13)
    base = jnp.clip(jax.random.normal(key, (VOCAB, D), jnp.float32), -4.0, 4.0)
    spread = jnp.exp(jax.random.uniform(jax.random.fold_in(key, 1), (VOCAB, 1), jnp.float32, 0.0, 2.3))
    values = base * spread * D ** (-0.5)
    return values.astype(jnp.bfloat16)


def plant(values, stream_key, least, high):
    dims = values.shape
    spot = [jax.random.randint(jax.random.fold_in(stream_key, axis), (), 0, dims[axis]) for axis in range(len(dims))]
    values = values.at[tuple(spot)].set(least)
    longest = dims.index(max(dims))
    spot[longest] = (spot[longest] + 1) % dims[longest]
    return values.at[tuple(spot)].set(high)


def block_scale(stream_key, shape, cuts, smallest, high):
    def one(position, blocks):
        heights = jax.random.uniform(jax.random.fold_in(jax.random.fold_in(stream_key, 6), position), (blocks,), jnp.float32, smallest / len(cuts), high / len(cuts))
        return jnp.repeat(jnp.exp(heights), shape[position] // blocks).reshape((-1,) + (1,) * (len(shape) - position - 1))

    factor_of = one(*cuts[0])
    for cut in cuts[1:]:
        factor_of = factor_of * one(*cut)
    return factor_of


def assign_block(rng, own, number, rows, number_of, top, bound, lean):
    sequence = jax.random.permutation(rng, number_of)
    packed, common = shares(number_of, rows * top, bound, lean, True), shares(number_of, rows * top, bound, lean, False)
    places = jnp.arange(number_of)

    def named(tallies, rotation):
        used = int((tallies > 0).sum())
        fixed = max(1, used // 4)
        shifted = fixed + (places - fixed + rotation * (used - fixed)) % max(1, number_of - fixed)
        return jnp.zeros((number_of,), jnp.int32).at[sequence[jnp.where(places < fixed, places, shifted)]].set(jnp.asarray(tallies, jnp.int32))

    tallies = jnp.where(number % 4 == 0, named(packed, number // 4), named(common, number - number // 4 - 1))
    mixed = jax.random.permutation(jax.random.fold_in(own, 3), number_of)
    donor, taker = mixed[0:number_of // 2 * 2:2], mixed[1:number_of // 2 * 2:2]
    slack = jnp.minimum(tallies[donor] - 1, bound - tallies[taker]) // 2
    slack = jnp.where((donor == sequence[0]) | (taker == sequence[0]) | (tallies[taker] == 0), 0, jnp.maximum(slack, 0))
    shifted = jax.random.randint(jax.random.fold_in(own, 4), (number_of // 2,), 0, 1 << 20) % (slack + 1)
    tallies = tallies.at[donor].add(-shifted).at[taker].add(shifted)
    labels = jnp.searchsorted(jnp.cumsum(tallies), jnp.arange(rows * top), side="right").astype(jnp.int32)
    table = labels.reshape(top, rows).T
    table = table[jax.random.permutation(jax.random.fold_in(own, 1), rows)]
    rotation = jax.random.randint(jax.random.fold_in(own, 2), (rows, 1), 0, top)
    return jnp.take_along_axis(table, (jnp.arange(top)[None, :] + rotation) % top, axis=1)


def shares(amount, total, limit, slope, full):
    loads = [(1 << 20) // math.isqrt(rank ** slope) + 1 for rank in range(1, amount + 1)]
    largest = limit if full else min(limit, max(-(-total // amount), total * loads[0] // sum(loads)))
    least = 1 if total - largest >= amount - 1 else 0
    given, surplus = [largest] + [least] * (amount - 1), total - largest - least * (amount - 1)
    while surplus > 0:
        movable = [i for i in range(1, amount) if given[i] < largest] or [i for i in range(1, amount) if given[i] < limit]
        mass, budget = sum([loads[i] for i in movable]), surplus
        for i in movable:
            addition = min(limit - given[i], max(1, budget * loads[i] // mass), surplus)
            given[i] = given[i] + addition
            surplus = surplus - addition
    return np.array(given)


def gaussian(rng, extent, width, most, split=(), kind=jnp.bfloat16):
    level = block_scale(rng, extent, split, -0.22, 0.18) if split else 1.0
    array = jax.random.normal(rng, extent, jnp.float32) * width * level
    return jnp.minimum(jnp.maximum(array, -most), most).astype(kind)


def setup_inputs(seed: int = 0) -> dict:
    key_of = jax.random.split(jax.random.key(seed), 18)
    query = draw_query(jax.random.fold_in(key_of[17], 71), 0)
    new_kv = gaussian(key_of[1], (2, REQUESTS, NODES, KVH * HD), 1.0, 4.0, ((1, 128), (3, 2)))
    cache = draw_cache(jax.random.fold_in(key_of[17], 71), 0)
    cache_len = draw_cache_len(jax.random.fold_in(key_of[17], 71), 0)
    parents = draw_parents(jax.random.fold_in(key_of[17], 71), 0)
    hidden = gaussian(key_of[5], (TOKENS, D), 1.0, 6.0, ((0, 128), (1, 2)))
    moe_gain = jnp.clip(1.0 + 0.1 * jax.random.normal(key_of[6], (D,), jnp.float32), 0.5, 1.5)
    routes_keys = jax.random.split(jax.random.fold_in(key_of[7], 1), TOKENS // (NODES * REQ_DEV))
    routes_turns = jax.random.permutation(jax.random.fold_in(key_of[7], 3), TOKENS // (NODES * REQ_DEV))
    routes = jax.vmap(lambda own, number: assign_block(jax.random.fold_in(key_of[7], 2), own, number, NODES * REQ_DEV, EXPERTS, TOPK, CAP, 2))(routes_keys, routes_turns).reshape((TOKENS, TOPK))
    gates = jnp.clip(jnp.exp(math.log(1.0) - 2.9957323 * jax.random.uniform(key_of[8], (TOKENS, TOPK), jnp.float32) ** block_scale(key_of[8], (TOKENS, TOPK), ((0, 128),), -0.2, 0.2)), 0.05, 1.0)
    w_gate = gaussian(key_of[9], (EXPERTS, D, FF_WIN), D ** -0.5, 0.09375, ((0, 128), (2, 2)))
    w_up = gaussian(key_of[10], (EXPERTS, D, FF_WIN), D ** -0.5, 0.09375, ((0, 128), (2, 2)))
    w_down = gaussian(key_of[11], (EXPERTS, FF_WIN, D), FF_WIN ** -0.5, 0.21875, ((0, 128), (1, 2)))
    accept = plant(jax.random.randint(key_of[12], (REQUESTS,), 0, NODES), jax.random.fold_in(key_of[12], 1), 0, NODES - 1).astype(jnp.int32)
    final_gain = jnp.clip(1.0 + 0.1 * jax.random.normal(key_of[13], (D,), jnp.float32), 0.5, 1.5)
    medusa_w = gaussian(key_of[14], (MH, D, D), D ** -0.5, 0.09375, ((1, 256),))
    medusa_b = gaussian(key_of[15], (MH, D), 0.5, 3.0, ((1, 256),), jnp.float32)
    lm_head = draw_lm_head(jax.random.fold_in(key_of[17], 71), 0)
    return dict(query=query, new_kv=new_kv, cache=cache, cache_len=cache_len, parents=parents, hidden=hidden, moe_gain=moe_gain, routes=routes, gates=gates, w_gate=w_gate, w_up=w_up, w_down=w_down, accept=accept, final_gain=final_gain, medusa_w=medusa_w, medusa_b=medusa_b, lm_head=lm_head)


eps_norm = 1e-06

def ancestors(parent):
    count = parent.shape[-1]
    nodes = jnp.arange(count, dtype=jnp.int32)
    direct = (nodes[None, :] == parent[:, None]) | (nodes[None, :] == nodes[:, None])
    reach = direct.astype(jnp.float32)
    for level_index in range(max(1, (count - 1).bit_length())):
        reach = jnp.minimum(jnp.dot(reach, reach, precision=lax.Precision.HIGHEST), 1.0)
    return reach > 0.5

def tree_attention(query, new_keys, new_values, cache_keys, cache_values, length, parent):
    nodes = query.shape[0]
    kv_heads = cache_keys.shape[-1] // HD
    group = query.shape[-1] // HD // kv_heads
    keys = jnp.concatenate([cache_keys, new_keys], 0).reshape(-1, kv_heads, HD)
    values = jnp.concatenate([cache_values, new_values], 0).reshape(-1, kv_heads, HD)
    queries = query.reshape(nodes, kv_heads, group, HD)
    scores = jnp.einsum('nkgd,skd->kgns', queries.astype(jnp.float32), keys.astype(jnp.float32)) * HD ** (-0.5)
    places = jnp.arange(cache_keys.shape[0], dtype=jnp.int32)
    cache_seen = jnp.broadcast_to((places < length)[None, :], (nodes, cache_keys.shape[0]))
    visible = jnp.concatenate([cache_seen, ancestors(parent)], 1)
    scores = jnp.where(visible[None, None], scores, -jnp.inf)
    largest = lax.optimization_barrier(jnp.max(scores, -1, keepdims=True))
    expo = jnp.exp(scores - largest)
    weight = (expo / lax.optimization_barrier(jnp.sum(expo, -1, keepdims=True))).astype(jnp.bfloat16)
    mixed = jnp.einsum('kgns,skd->nkgd', weight.astype(jnp.float32), values.astype(jnp.float32))
    return mixed.astype(jnp.bfloat16).reshape(nodes, -1)

def rms_scaled(values_in, gain):
    values = values_in.astype(jnp.float32)
    factor = lax.rsqrt(lax.optimization_barrier(jnp.mean(values * values, -1, keepdims=True)) + eps_norm)
    return (values * factor * gain).astype(jnp.bfloat16)

def expert_ffn(inputs, gate_matrix, up_matrix, down_matrix):
    gate_part = jnp.dot(inputs, gate_matrix, preferred_element_type=jnp.float32)
    up_part = jnp.dot(inputs, up_matrix, preferred_element_type=jnp.float32)
    activation = (jax.nn.silu(gate_part) * up_part).astype(jnp.bfloat16)
    return jnp.dot(activation, down_matrix, preferred_element_type=jnp.float32)

def reference(query, new_kv, cache, cache_len, parents, hidden, moe_gain, routes, gates, w_gate, w_up, w_down, accept, final_gain, medusa_w, medusa_b, lm_head):
    attended = jax.vmap(tree_attention)(query, new_kv[0], new_kv[1], cache[0], cache[1], cache_len, parents)
    normed = rms_scaled(hidden, moe_gain)
    tokens_dev = NODES * REQ_DEV
    picks = routes.reshape(N_EP, tokens_dev * TOPK)
    onehot = (picks[:, :, None] == jnp.arange(EXPERTS, dtype=jnp.int32)[None, None, :]).astype(jnp.int32)
    ranking = lax.optimization_barrier(jnp.sum(jnp.cumsum(onehot, 1) * onehot, -1)) - 1
    slot_index = jnp.arange(N_EP, dtype=jnp.int32)[:, None] * CAP + ranking
    owner = (jnp.arange(TOKENS * TOPK, dtype=jnp.int32) // TOPK).astype(jnp.int32)
    share = gates / lax.optimization_barrier(jnp.sum(gates, -1, keepdims=True))
    table = jnp.full((EXPERTS, N_EP * CAP), -1, jnp.int32).at[picks.reshape(-1), slot_index.reshape(-1)].set(owner)
    share_table = jnp.zeros((EXPERTS, N_EP * CAP), jnp.float32).at[picks.reshape(-1), slot_index.reshape(-1)].set(share.reshape(-1))

    def one_expert(total, pieces):
        gate_matrix, up_matrix, down_matrix, owners, weights = pieces
        safe = jnp.maximum(owners, 0)
        inputs = jnp.where((owners >= 0)[:, None], normed[safe], jnp.zeros((), jnp.bfloat16))
        output = expert_ffn(inputs, gate_matrix, up_matrix, down_matrix).astype(jnp.bfloat16)
        return (total.at[safe].add(weights[:, None] * output.astype(jnp.float32)), None)
    total, unused = lax.scan(one_expert, jnp.zeros((TOKENS, D), jnp.float32), (w_gate, w_up, w_down, table, share_table))
    layer_out = (hidden.astype(jnp.float32) + total).astype(jnp.bfloat16)
    chosen = layer_out.reshape(REQUESTS, NODES, D)[jnp.arange(REQUESTS), accept]
    final = rms_scaled(chosen, final_gain)
    inner = jnp.einsum('ri,koi->kro', final.astype(jnp.float32), medusa_w.astype(jnp.float32))
    heads = (final.astype(jnp.float32)[None] + jax.nn.silu(inner + medusa_b[:, None, :])).astype(jnp.bfloat16)
    logits = jnp.einsum('krd,vd->krv', heads.astype(jnp.float32), lm_head.astype(jnp.float32))
    largest = lax.optimization_barrier(jnp.max(logits, -1, keepdims=True))
    totals = lax.optimization_barrier(jnp.sum(jnp.exp(logits - largest), -1, keepdims=True))
    logprob = logits - largest - jnp.log(totals)
    return (attended, layer_out, logprob)
```

```python
import jax
import jax.numpy as jnp
from jax import lax
from jax.sharding import Mesh, PartitionSpec as P

HD = 128
TOPK = 8
NODES = 32
CAP = 4
EXPERTS = 128
D = 4096
HALF = D // 2

eps_norm = 1e-06
EP = ("x", "z", "y")
TP = "c"
ALL = ("x", "z", "y", "c")
SWAP = [(0, 1), (1, 0)]


def ancestors(parent):
    count = parent.shape[-1]
    nodes = jnp.arange(count, dtype=jnp.int32)
    direct = (nodes[None, :] == parent[:, None]) | (nodes[None, :] == nodes[:, None])
    reach = direct.astype(jnp.float32)
    for level_index in range(max(1, (count - 1).bit_length())):
        reach = jnp.minimum(jnp.dot(reach, reach, precision=lax.Precision.HIGHEST), 1.0)
    return reach > 0.5


def tree_attention(query, new_keys, new_values, cache_keys, cache_values, length, parent):
    nodes = query.shape[0]
    kv_heads = cache_keys.shape[-1] // HD
    group = query.shape[-1] // HD // kv_heads
    keys = jnp.concatenate([cache_keys, new_keys], 0).reshape(-1, kv_heads, HD)
    values = jnp.concatenate([cache_values, new_values], 0).reshape(-1, kv_heads, HD)
    queries = query.reshape(nodes, kv_heads, group, HD)
    scores = jnp.einsum(
        "nkgd,skd->kgns", queries, keys, preferred_element_type=jnp.float32
    ) * HD ** (-0.5)
    places = jnp.arange(cache_keys.shape[0], dtype=jnp.int32)
    cache_seen = jnp.broadcast_to((places < length)[None, :], (nodes, cache_keys.shape[0]))
    visible = jnp.concatenate([cache_seen, ancestors(parent)], 1)
    scores = jnp.where(visible[None, None], scores, -jnp.inf)
    largest = jnp.max(scores, -1, keepdims=True)
    expo = jnp.exp(scores - largest)
    weight = (expo / jnp.sum(expo, -1, keepdims=True)).astype(jnp.bfloat16)
    mixed = jnp.einsum("kgns,skd->nkgd", weight, values, preferred_element_type=jnp.float32)
    return mixed.astype(jnp.bfloat16).reshape(nodes, -1)


def swap(value):
    return lax.ppermute(value, TP, SWAP)


def spread(value, axes, count):
    copies = jnp.broadcast_to(value[None], (count,) + value.shape)
    return lax.all_to_all(copies, axes, 0, 0, tiled=True)


def pair(index, own, other, axis):
    first = jnp.where(index == 0, own, other)
    second = jnp.where(index == 0, other, own)
    return jnp.concatenate([first, second], axis)


def dot32(left, right):
    return jnp.dot(left, right, preferred_element_type=jnp.float32)


def own_scaled(own, square_sum, own_gain):
    factor = lax.rsqrt(square_sum / D + eps_norm)
    return (own * factor * own_gain).astype(jnp.bfloat16)


def merged(stats):
    tops, sums = stats[:, :2], stats[:, 2:]
    top = jnp.max(tops, 0)
    return jnp.concatenate([top, jnp.sum(sums * jnp.exp(tops - top[None]), 0)], 0)


def on_device(
    query,
    new_kv,
    cache,
    cache_len,
    parents,
    hidden,
    moe_gain,
    routes,
    gates,
    w_gate,
    w_up,
    w_down,
    accept,
    final_gain,
    medusa_w,
    medusa_b,
    lm_head,
):
    core = lax.axis_index(TP)
    own_at, other_at = core * HALF, (1 - core) * HALF

    def own_half(array, axis):
        return lax.dynamic_slice_in_dim(array, own_at, HALF, axis)

    def other_half(array, axis):
        return lax.dynamic_slice_in_dim(array, other_at, HALF, axis)

    attended = jax.vmap(tree_attention)(
        query, new_kv[0], new_kv[1], cache[0], cache[1], cache_len, parents
    )

    down_own = own_half(w_down[0], 1)
    down_other = swap(other_half(w_down[0], 1))

    rows = hidden.astype(jnp.float32)
    squares = lax.psum(jnp.sum(rows * rows, -1, keepdims=True), TP)
    normed = own_scaled(rows, squares, own_half(moe_gain, 0))

    picks = routes.reshape(-1)
    onehot = picks[:, None] == jnp.arange(EXPERTS, dtype=jnp.int32)[None, :]
    onehot = onehot.astype(jnp.int32)
    ranking = jnp.sum(jnp.cumsum(onehot, 0) * onehot, -1) - 1
    slot_index = (picks * CAP + ranking).reshape(NODES, TOPK)
    places = jnp.arange(EXPERTS * CAP, dtype=jnp.int32)[:, None, None] == slot_index[None]
    chooser = jnp.any(places, -1).astype(jnp.bfloat16)
    outgoing = dot32(chooser, normed).astype(jnp.bfloat16).reshape(EXPERTS, CAP, HALF)
    arrived = lax.all_to_all(outgoing, EP, 0, 0, tiled=True).reshape(EXPERTS * CAP, HALF)
    arrived_other = swap(arrived)

    gate_part = dot32(arrived, own_half(w_gate[0], 0)) + dot32(
        arrived_other, other_half(w_gate[0], 0)
    )
    up_part = dot32(arrived, own_half(w_up[0], 0)) + dot32(arrived_other, other_half(w_up[0], 0))
    activation = (jax.nn.silu(gate_part) * up_part).astype(jnp.bfloat16)
    finished = dot32(activation, down_own) + dot32(swap(activation), down_other)
    finished = finished.astype(jnp.bfloat16).reshape(EXPERTS, CAP, HALF)
    returned = lax.all_to_all(finished, EP, 0, 0, tiled=True).reshape(EXPERTS * CAP, HALF)

    share = gates / jnp.sum(gates, -1, keepdims=True)
    picked_out = returned[slot_index.reshape(-1)].reshape(NODES, TOPK, HALF)
    mixture = jnp.sum(share[:, :, None] * picked_out.astype(jnp.float32), 1)
    layer_out = (rows + mixture).astype(jnp.bfloat16)

    chosen = layer_out[accept[0]].reshape(16, 128)
    chosen_own = spread(chosen, EP, EXPERTS).reshape(EXPERTS, HALF)
    chosen_other = swap(chosen_own)
    wide_own, wide_other = chosen_own.astype(jnp.float32), chosen_other.astype(jnp.float32)
    squares = jnp.sum(wide_own * wide_own, -1, keepdims=True) + jnp.sum(
        wide_other * wide_other, -1, keepdims=True
    )
    final = pair(
        core,
        own_scaled(wide_own, squares, own_half(final_gain, 0)),
        own_scaled(wide_other, squares, other_half(final_gain, 0)),
        1,
    )
    block = medusa_w.shape[1]
    index = (lax.axis_index("x") * 8 + lax.axis_index("z")) * 4 + lax.axis_index("y")
    offset = (index * 2 + core) * block
    inner = jnp.einsum("koi,ri->kor", medusa_w, final, preferred_element_type=jnp.float32)
    own_part = lax.dynamic_slice_in_dim(final, offset, block, 1).astype(jnp.float32).T
    head_part = own_part[None] + jax.nn.silu(inner + medusa_b[:, :, None])
    head_part = head_part.astype(jnp.bfloat16).reshape(2 * block, EXPERTS)

    heads_own = spread(head_part, EP, EXPERTS)
    heads_other = swap(heads_own)
    both = pair(core, heads_own[:, None], heads_other[:, None], 1)
    both = both.reshape(EXPERTS, 2, 2, block, EXPERTS)
    heads = jnp.transpose(both, (2, 0, 1, 3, 4)).reshape(2, D, EXPERTS)
    logits = jnp.einsum("kdr,vd->krv", heads, lm_head, preferred_element_type=jnp.float32)
    top = jnp.max(logits, -1)
    sums = jnp.sum(jnp.exp(logits - top[..., None]), -1)
    stats = jnp.concatenate([top, sums], 0)
    stats = merged(spread(stats, ("x", "y", "c"), 32))
    stats = merged(spread(stats, "z", 8))
    logprob = logits - (stats[:2] + jnp.log(stats[2:]))[..., None]
    return (attended, layer_out, logprob)


def solution(mesh):
    fine = Mesh(mesh.devices.reshape(4, 8, 4, 2), ALL)
    in_specs = (
        P(EP, None, TP),
        P(None, EP, None, TP),
        P(None, EP, None, TP),
        P(EP),
        P(EP, None),
        P(EP, TP),
        P(),
        P(EP, None),
        P(EP, None),
        P(EP, None, TP),
        P(EP, None, TP),
        P(EP, TP, None),
        P(EP),
        P(),
        P(None, ALL, None),
        P(None, ALL),
        P(ALL, None),
    )
    out_specs = (P(EP, None, TP), P(EP, TP), P(None, None, ALL))
    return jax.shard_map(
        on_device, mesh=fine, in_specs=in_specs, out_specs=out_specs, check_vma=False
    )
```

```python
import jax
import jax.numpy as jnp
from jax import lax
from jax.experimental import pallas as pl
from jax.experimental.pallas import tpu as pltpu
from jax.sharding import Mesh, PartitionSpec as P

HD = 128
TOPK = 8
NODES = 32
CAP = 4
EXPERTS = 128
D = 4096
HALF = D // 2

eps_norm = 1e-06
EP = ("x", "z", "y")
TP = "c"
ALL = ("x", "z", "y", "c")
PLANE = ("x", "y")
NZ = 8
NY = 4
NPLANE = 16
LANES = 128
BLOCK = 512
VMEM_LIMIT = 40 << 20
SWAP = [(0, 1), (1, 0)]


def swap(value):
    return lax.ppermute(value, TP, SWAP)


def around(count, step):
    return [(chip, (chip + step) % count) for chip in range(count)]


def exchange(value, axes):
    return lax.all_to_all(value, axes, 0, 0, tiled=True)


def dot32(left, right):
    return jnp.dot(left, right, preferred_element_type=jnp.float32)


def last_dot(left, right):
    return lax.dot_general(
        left, right, (((1,), (1,)), ((), ())), preferred_element_type=jnp.float32
    )


def first_dot(left, right):
    return lax.dot_general(
        left, right, (((0,), (0,)), ((), ())), preferred_element_type=jnp.float32
    )


def iota(shape, dim):
    return lax.broadcasted_iota(jnp.int32, shape, dim)


def as_bf16(mask):
    return mask.astype(jnp.float32).astype(jnp.bfloat16)


def as_column(row):
    count = row.shape[1]
    here = iota((count, count), 0) == iota((count, count), 1)
    return jnp.sum(jnp.where(here, row, 0.0), 1, keepdims=True)


def silu(value):
    return value / (1.0 + jnp.exp(-value))


SMEM = pl.BlockSpec(memory_space=pltpu.SMEM)
ANY = pl.BlockSpec(memory_space=pl.ANY)


def whole(array):
    return pl.BlockSpec(array.shape, lambda *_: (0,) * len(array.shape))


def in_hbm(array):
    return pltpu.with_memory_space_constraint(array, pltpu.HBM)


def like(shape, dtype):
    return jax.ShapeDtypeStruct(shape, dtype)


def call(kernel, scalars, arrays, out_shape, flops=0, moved=1 << 20, unused=(), scratch=()):
    outs = out_shape if isinstance(out_shape, (list, tuple)) else [out_shape]
    count = len(scalars)

    def body(*refs):
        rest = refs[count + len(arrays) + len(unused) :]
        kernel(*refs[: count + len(arrays)], *rest)

    result = pl.pallas_call(
        body,
        out_shape=list(outs),
        in_specs=[SMEM] * count + [whole(a) for a in arrays] + [ANY] * len(unused),
        out_specs=[whole(o) for o in outs],
        scratch_shapes=list(scratch),
        compiler_params=pltpu.CompilerParams(vmem_limit_bytes=VMEM_LIMIT),
        cost_estimate=pl.CostEstimate(flops=flops, bytes_accessed=moved, transcendentals=0),
    )(*scalars, *arrays, *unused)
    return result if isinstance(out_shape, (list, tuple)) else result[0]


def attention_kernel(length, query, new_kv, cache, parents, attended):
    nodes = query.shape[1]
    heads = query.shape[2] // HD
    kv_heads = cache.shape[3] // HD
    group = heads // kv_heads
    shape = (nodes, nodes)
    parent = as_column(parents[...].astype(jnp.float32))
    column = iota(shape, 1).astype(jnp.float32)
    reach = ((column == parent) | (iota(shape, 0) == iota(shape, 1))).astype(jnp.float32)
    for _ in range(5):
        reach = jnp.minimum(dot32(reach.astype(jnp.bfloat16), reach.astype(jnp.bfloat16)), 1.0)
    reach = jnp.concatenate([reach] * group, 0)
    for kv in range(kv_heads):
        here = pl.ds(kv * HD, HD)
        first = kv * group
        rows = [query[0, :, (first + h) * HD : (first + h + 1) * HD] for h in range(group)]
        rows = jnp.concatenate(rows, 0)
        old = last_dot(rows, cache[0, 0, :, here]) * HD ** (-0.5)
        new = last_dot(rows, new_kv[0, 0, :, here]) * HD ** (-0.5)
        old = jnp.where(iota(old.shape, 1) < length[0], old, -jnp.inf)
        new = jnp.where(reach > 0.5, new, -jnp.inf)
        top = jnp.maximum(jnp.max(old, -1, keepdims=True), jnp.max(new, -1, keepdims=True))
        old, new = jnp.exp(old - top), jnp.exp(new - top)
        total = jnp.sum(old, -1, keepdims=True) + jnp.sum(new, -1, keepdims=True)
        mixed = dot32((old / total).astype(jnp.bfloat16), cache[1, 0, :, here])
        mixed = mixed + dot32((new / total).astype(jnp.bfloat16), new_kv[1, 0, :, here])
        mixed = mixed.astype(jnp.bfloat16)
        for h in range(group):
            attended[0, :, (first + h) * HD : (first + h + 1) * HD] = mixed[
                h * nodes : (h + 1) * nodes
            ]


def begin_kernel(accept, hidden, routes, gates, weights, bias, squares, notes, wide):
    rows = hidden[...].astype(jnp.float32)
    squares[...] = jnp.broadcast_to(jnp.sum(rows * rows, -1, keepdims=True), squares.shape)
    share = gates[...] / jnp.sum(gates[...], 0, keepdims=True)
    share_hi = share.astype(jnp.bfloat16).astype(jnp.float32)
    flag = (iota((TOPK, NODES), 1) == accept[0]).astype(jnp.float32)
    stack = [routes[...].astype(jnp.float32), share_hi, share - share_hi, flag]
    stack = jnp.concatenate(stack, 0).astype(jnp.bfloat16)
    places = as_bf16(iota((NODES, LANES), 0) == iota((NODES, LANES), 1))
    notes[...] = first_dot(stack, places).astype(jnp.bfloat16)
    block = weights.shape[1]
    lane = iota((block, LANES), 1)
    for head in range(2):
        wide[head, :, :D] = weights[head]
        value = as_column(bias[head : head + 1, :])
        extra = jnp.zeros((block, LANES), jnp.float32)
        for place in range(3):
            part = value.astype(jnp.bfloat16).astype(jnp.float32)
            extra = jnp.where(lane == place, part, extra)
            value = value - part
        wide[head, :, D:] = extra.astype(jnp.bfloat16)


def assemble_kernel(core, my_y, *refs):
    own, other, weights = refs[:NY], refs[NY], refs[NY + 1]
    block = own[0].shape[1]
    for step in range(NY):
        place = lax.rem(my_y[0] - step + NY, NY) * 2
        for head in range(2):
            here = pl.ds(pl.multiple_of((place + core[0]) * block, block), block)
            weights[head, here, :] = own[step][head]
            here = pl.ds(pl.multiple_of((place + 1 - core[0]) * block, block), block)
            weights[head, here, :] = other[step, head]


def pack_kernel(core, hidden, squares, gain, notes, packet):
    factor = lax.rsqrt(squares[...][:, :1] / D + eps_norm)
    own_gain = jnp.where(core[0] == 0, gain[:HALF], gain[HALF:]).reshape(1, HALF)
    normed = (hidden[...].astype(jnp.float32) * factor * own_gain).astype(jnp.bfloat16)
    for chip in range(NZ):
        packet[chip, :, :HALF] = normed
        packet[chip, :, HALF:] = notes[...]


def route_kernel(my_z, column, outgoing, mix_hi, mix_lo, accepted_mix):
    count = NZ * NODES
    slots = NZ * CAP
    tokens = column[...].reshape(count, HALF + LANES)
    turn = as_bf16(iota((NODES, LANES), 0) == iota((NODES, LANES), 1))
    notes = last_dot(turn, tokens[:, HALF:])
    expert = iota((NPLANE, 1), 0)
    expert = (((expert // 4) * NZ + my_z[0]) * 4 + expert % 4).astype(jnp.float32)
    member = jnp.zeros((NPLANE, count), jnp.float32)
    share_hi, share_lo = member, member
    for pick in range(TOPK):
        match = (notes[pick : pick + 1] == expert).astype(jnp.float32)
        member = member + match
        share_hi = share_hi + match * notes[TOPK + pick : TOPK + pick + 1]
        share_lo = share_lo + match * notes[2 * TOPK + pick : 2 * TOPK + pick + 1]
    first, second = iota((count, count), 0), iota((count, count), 1)
    earlier = (first < second) & (first // NODES == second // NODES)
    rank = dot32(member.astype(jnp.bfloat16), as_bf16(earlier))
    source = iota((1, count), 1) // NODES
    slot = jnp.where(member > 0.5, (source * CAP).astype(jnp.float32) + rank, -1.0)
    wanted = iota((slots, 1), 0).astype(jnp.float32)
    chosen = []
    for place in range(NPLANE):
        one = (slot[place : place + 1] == wanted).astype(jnp.float32)
        here = pl.ds(place * slots, slots)
        mix_hi[here, :] = (one * share_hi[place : place + 1]).astype(jnp.bfloat16)
        mix_lo[here, :] = (one * share_lo[place : place + 1]).astype(jnp.bfloat16)
        chosen.append(one.astype(jnp.bfloat16))
    chosen = jnp.concatenate(chosen, 0)
    for piece in range(HALF // BLOCK):
        here = slice(piece * BLOCK, (piece + 1) * BLOCK)
        part = dot32(chosen, tokens[:, here]).astype(jnp.bfloat16)
        outgoing[:, :, here] = part.reshape(NPLANE, slots, BLOCK)
    flag = notes[3 * TOPK : 3 * TOPK + 1]
    accepted = jnp.where(source == iota((NZ, 1), 0), flag, 0.0).astype(jnp.bfloat16)
    accepted_mix[:NZ] = last_dot(accepted, mix_hi[...]).astype(jnp.bfloat16)
    accepted_mix[NZ:] = last_dot(accepted, mix_lo[...]).astype(jnp.bfloat16)


def half_sums(core, rows, w_gate, w_up):
    here = pl.ds(pl.multiple_of(core * HALF, HALF), HALF)
    rows = rows[...].reshape(-1, HALF)
    return dot32(rows, w_gate[0, here, :]), dot32(rows, w_up[0, here, :])


def first_half_kernel(core, rows, w_gate, w_up, gate, up):
    gate[...], up[...] = half_sums(core[0], rows, w_gate, w_up)


def second_half_kernel(core, rows, w_gate, w_up, gate, up, activation):
    gate_part, up_part = half_sums(1 - core[0], rows, w_gate, w_up)
    activation[...] = (silu(gate[...] + gate_part) * (up[...] + up_part)).astype(jnp.bfloat16)


def down_kernel(core, own, other, down, other_down, finished):
    del core
    rows = jnp.concatenate([own[...], other[...]], 1)
    part = dot32(rows, jnp.concatenate([down[0], other_down[...]], 0))
    finished[...] = part.astype(jnp.bfloat16).reshape(finished.shape)


def down(core, own, other, w_down, other_down, out_shape):
    rows, units = own.shape
    steps = HALF // BLOCK
    column = lambda i, core: (0, i)
    return pl.pallas_call(
        down_kernel,
        out_shape=out_shape,
        grid_spec=pltpu.PrefetchScalarGridSpec(
            num_scalar_prefetch=1,
            grid=(steps,),
            in_specs=[
                pl.BlockSpec((rows, units), lambda i, core: (0, 0)),
                pl.BlockSpec((rows, units), lambda i, core: (0, 0)),
                pl.BlockSpec((1, units, BLOCK), lambda i, core: (0, 0, core[0] * steps + i)),
                pl.BlockSpec((units, BLOCK), column),
            ],
            out_specs=pl.BlockSpec((NPLANE, NZ * CAP, BLOCK), lambda i, core: (0, 0, i)),
        ),
        compiler_params=pltpu.CompilerParams(vmem_limit_bytes=VMEM_LIMIT),
        cost_estimate=pl.CostEstimate(
            flops=4 * rows * HALF * units, bytes_accessed=6 << 20, transcendentals=0
        ),
    )(core, own, other, w_down, other_down)


def accepted_kernel(accept, my_z, mix, returned, hidden, parts):
    part = dot32(mix[...], returned[...].reshape(-1, HALF))
    part = part[:NZ] + part[NZ:]
    here = iota((NODES, 1), 0) == accept[0]
    own = jnp.sum(jnp.where(here, hidden[...].astype(jnp.float32), 0.0), 0, keepdims=True)
    part = part + jnp.where(iota((NZ, 1), 0) == my_z[0], own, 0.0)
    part = part.astype(jnp.bfloat16)
    for place in range(2 * NZ):
        parts[place] = part


def mixture_kernel(my_z, mix_hi, mix_lo, returned, *refs):
    outs, partial = refs[:NZ], refs[NZ]
    rows = returned[...].reshape(-1, HALF)
    partial[...] = first_dot(mix_hi[...], rows) + first_dot(mix_lo[...], rows)
    for step in range(NZ):
        place = lax.rem(my_z[0] + step, NZ)
        block = partial[pl.ds(pl.multiple_of(place * NODES, NODES), NODES), :]
        outs[step][...] = block.astype(outs[step].dtype)


def final_kernel(parts, gain, copies):
    chosen = jnp.sum(parts[...].reshape(NZ, 2, NZ, HALF).astype(jnp.float32), 0)
    chosen = chosen.astype(jnp.bfloat16).astype(jnp.float32)
    squares = jnp.sum(chosen * chosen, -1, keepdims=True)
    factor = lax.rsqrt((squares[0] + squares[1]) / D + eps_norm)
    for half in range(2):
        final = (chosen[half] * factor * gain[half * HALF : (half + 1) * HALF].reshape(1, HALF)).astype(jnp.bfloat16)
        for chip in range(copies.shape[0]):
            copies[chip, :, half * HALF : (half + 1) * HALF] = final


def medusa_kernel(core, tile, final, weights, copies):
    count = 4 * NZ
    shape = (count // 2, count)
    row = iota(shape, 0)
    pick = as_bf16(iota(shape, 1) == row // 4 * NZ + core[0] * 4 + row % 4)
    rows = dot32(pick, final[...].reshape(count, D)).astype(jnp.bfloat16)
    here = pl.ds(pl.multiple_of(tile[0] * LANES, LANES), LANES)
    own = dot32(pick, final[:, :, here].reshape(count, LANES))
    ones = as_bf16(iota((count // 2, LANES), 1) < 3)
    rows = jnp.concatenate([rows, ones], 1)
    heads = [own + silu(last_dot(rows, weights[head])) for head in range(2)]
    heads = jnp.concatenate(heads, 0).astype(jnp.bfloat16)
    for chip in range(NZ):
        copies[chip] = heads


def copy_kernel(heads, copies):
    for chip in range(NPLANE):
        copies[chip] = heads[...]


def head_sums(heads, lm):
    tiles = []
    for x in range(4):
        for z in range(NZ):
            tiles.append(jnp.concatenate([heads[x * NY + y, z] for y in range(NY)], 0))
    return last_dot(lm[...], jnp.concatenate(tiles, 1))


def first_logits_kernel(heads, lm, total):
    total[...] = head_sums(heads, lm)


def logits_kernel(core, heads, lm, before, logits, stats):
    both = jnp.concatenate([before[...], head_sums(heads, lm)], 1)
    shape = (2 * EXPERTS, 2 * EXPERTS)
    lane = iota(shape, 0)
    z = jnp.where(lane < EXPERTS, core[0], 1 - core[0]) * 4 + lane % 4
    wanted = lane // 16 % 2 * EXPERTS + lane // 4 % 4 * 32 + z * 4 + lane // 32 % 4
    order = as_bf16(wanted == iota(shape, 1))
    total = jnp.zeros(both.shape, jnp.float32)
    for _ in range(3):
        part = both.astype(jnp.bfloat16)
        total = total + dot32(part, order)
        both = both - part.astype(jnp.float32)
    top = jnp.max(total, 0, keepdims=True)
    sums = jnp.sum(jnp.exp(total - top), 0, keepdims=True)
    for head in range(2):
        here = slice(head * EXPERTS, (head + 1) * EXPERTS)
        logits[head] = total[:, here]
        for place in range(stats.shape[0]):
            stats[place, head : head + 1, :] = top[:, here]
            stats[place, 2 + head : 3 + head, :] = sums[:, here]


def merged(stats):
    tops, sums = stats[:, :2], stats[:, 2:]
    top = jnp.max(tops, 0)
    return top, jnp.sum(sums * jnp.exp(tops - top[None]), 0)


def merge_kernel(stats, copies):
    top, sums = merged(stats[...])
    for chip in range(NZ):
        copies[chip, :2, :] = top
        copies[chip, 2:, :] = sums


def finish_kernel(stats, logits, logprob):
    top, sums = merged(stats[...])
    shift = top + jnp.log(sums)
    for head in range(2):
        logprob[head] = logits[head] - shift[head : head + 1, :]


def on_device(
    query,
    new_kv,
    cache,
    cache_len,
    parents,
    hidden,
    moe_gain,
    routes,
    gates,
    w_gate,
    w_up,
    w_down,
    accept,
    final_gain,
    medusa_w,
    medusa_b,
    lm_head,
):
    bf16, f32 = jnp.bfloat16, jnp.float32
    core, my_z = lax.axis_index(TP), lax.axis_index("z")
    core_at, z_at, y_at = core.reshape(1), my_z.reshape(1), lax.axis_index("y").reshape(1)
    tile_at = (lax.axis_index("x") * NZ + my_z).reshape(1)
    slots = NPLANE * NZ * CAP
    units = w_gate.shape[2]
    vocab = lm_head.shape[0]

    squares, notes, wide_w = call(
        begin_kernel,
        [accept],
        [in_hbm(array) for array in (hidden, routes.T, gates.T, medusa_w, medusa_b)],
        [
            like((NODES, LANES), f32),
            like((NODES, LANES), bf16),
            like(medusa_w.shape[:2] + (D + LANES,), bf16),
        ],
    )

    packet = call(
        pack_kernel,
        [core_at],
        [in_hbm(hidden), lax.psum(squares, TP), in_hbm(moe_gain), notes],
        pltpu.HBM((NZ, NODES, HALF + LANES), bf16),
    )
    column = exchange(packet, "z")

    attended = call(
        attention_kernel,
        [cache_len],
        [query, new_kv, cache, parents],
        like(query.shape, bf16),
        flops=4 << 24,
        moved=4 << 20,
    )
    wide = [wide_w] + [lax.ppermute(wide_w, "y", around(NY, step)) for step in range(1, NY)]
    block_w = call(
        assemble_kernel,
        [core_at, y_at],
        wide + [swap(jnp.stack(wide))],
        pltpu.HBM((2, LANES, D + LANES), bf16),
        moved=4 << 20,
    )
    other_down = swap(lax.dynamic_slice_in_dim(w_down[0], (1 - core) * HALF, HALF, 1))

    outgoing, mix_hi, mix_lo, accepted_mix = call(
        route_kernel,
        [z_at],
        [column],
        [
            pltpu.VMEM((NPLANE, NZ * CAP, HALF), bf16),
            like((slots, NZ * NODES), bf16),
            like((slots, NZ * NODES), bf16),
            like((2 * NZ, slots), bf16),
        ],
        flops=2 * slots * NZ * NODES * HALF,
        moved=4 << 20,
        unused=[attended, in_hbm(block_w), in_hbm(other_down)],
    )
    arrived = exchange(outgoing, PLANE)
    sums = call(
        first_half_kernel,
        [core_at],
        [arrived, w_gate, w_up],
        [like((slots, units), f32)] * 2,
        flops=4 * slots * HALF * units,
        moved=8 << 20,
    )
    activation = call(
        second_half_kernel,
        [core_at],
        [swap(arrived), w_gate, w_up, *sums],
        like((slots, units), bf16),
        flops=4 * slots * HALF * units,
        moved=8 << 20,
    )
    finished = down(
        core_at,
        activation,
        swap(activation),
        w_down,
        other_down,
        pltpu.VMEM((NPLANE, NZ * CAP, HALF), bf16),
    )
    returned = exchange(finished, PLANE)

    parts = call(
        accepted_kernel,
        [accept, z_at],
        [accepted_mix, returned, hidden],
        pltpu.HBM((2 * NZ, NZ, HALF), bf16),
        flops=4 * NZ * slots * HALF,
        moved=3 << 20,
    )
    parts = exchange(parts, ("z", "c"))
    own, *others = call(
        mixture_kernel,
        [z_at],
        [mix_hi, mix_lo, returned],
        [like((NODES, HALF), f32)] + [like((NODES, HALF), bf16)] * (NZ - 1),
        flops=4 * slots * NZ * NODES * HALF,
        moved=6 << 20,
        scratch=[pltpu.VMEM((NZ * NODES, HALF), f32)],
    )
    sent = {}
    for step, other in enumerate(others, 1):
        sent[step] = lax.ppermute(other, "z", around(NZ, step))

    final = call(
        final_kernel,
        [],
        [parts, in_hbm(final_gain)],
        pltpu.HBM((4, NZ, D), bf16),
        unused=[own],
    )
    final = exchange(final, "x")
    heads = call(
        medusa_kernel,
        [core_at, tile_at],
        [final, block_w],
        pltpu.HBM((NZ, 32, LANES), bf16),
        flops=2 * 16 * D * 256,
        moved=3 << 20,
        unused=[sent[step] for step in (1, 7, 2)],
    )
    heads = exchange(heads, "z")
    heads = call(
        copy_kernel,
        [],
        [heads],
        pltpu.HBM((NPLANE, NZ, 32, LANES), bf16),
        unused=[sent[step] for step in (6, 3, 5, 4)],
    )
    heads = exchange(heads, PLANE)
    total = call(
        first_logits_kernel,
        [],
        [heads, lm_head],
        like((vocab, EXPERTS), f32),
        flops=2 * EXPERTS * D * vocab,
        moved=4 << 20,
    )
    logits, stats = call(
        logits_kernel,
        [core_at],
        [swap(heads), lm_head, total],
        [like((2, vocab, EXPERTS), f32), pltpu.HBM((32, 4, EXPERTS), f32)],
        flops=2 * EXPERTS * D * vocab,
        moved=4 << 20,
    )
    mixture = own
    for other in sent.values():
        mixture = mixture + other.astype(f32)
    layer_out = (hidden.astype(f32) + mixture).astype(bf16)
    stats = exchange(stats, ("x", "y", "c"))
    stats = call(merge_kernel, [], [stats], pltpu.HBM((NZ, 4, EXPERTS), f32))
    stats = exchange(stats, "z")
    logprob = call(finish_kernel, [], [stats, logits], like((2, vocab, EXPERTS), f32))
    return (attended, layer_out, jnp.transpose(logprob, (0, 2, 1)))


def solution(mesh):
    fine = Mesh(mesh.devices.reshape(4, 8, 4, 2), ALL)
    in_specs = (
        P(EP, None, TP),
        P(None, EP, None, TP),
        P(None, EP, None, TP),
        P(EP),
        P(EP, None),
        P(EP, TP),
        P(),
        P(EP, None),
        P(EP, None),
        P(EP, None, TP),
        P(EP, None, TP),
        P(EP, TP, None),
        P(EP),
        P(),
        P(None, ALL, None),
        P(None, ALL),
        P(ALL, None),
    )
    out_specs = (P(EP, None, TP), P(EP, TP), P(None, None, ALL))
    return jax.shard_map(
        on_device, mesh=fine, in_specs=in_specs, out_specs=out_specs, check_vma=False
    )
```

```python
import jax
import jax.numpy as jnp
from jax import lax
from jax.experimental import pallas as pl
from jax.experimental.pallas import tpu as pltpu
from jax.sharding import Mesh, PartitionSpec as P

HD = 128
TOPK = 8
NODES = 32
CAP = 4
EXPERTS = 128
D = 4096
HALF = D // 2

eps_norm = 1e-06
EP = ("x", "z", "y")
TP = "c"
ALL = ("x", "z", "y", "c")
PLANE = ("x", "y")
NZ = 8
NY = 4
NPLANE = 16
LANES = 128
BLOCK = 512
VMEM_LIMIT = 40 << 20
SWAP = [(0, 1), (1, 0)]


def swap(value):
    return lax.ppermute(value, TP, SWAP)


def around(count, step):
    return [(chip, (chip + step) % count) for chip in range(count)]


def exchange(value, axes):
    return lax.all_to_all(value, axes, 0, 0, tiled=True)


def dot32(left, right):
    return jnp.dot(left, right, preferred_element_type=jnp.float32)


def last_dot(left, right):
    return lax.dot_general(
        left, right, (((1,), (1,)), ((), ())), preferred_element_type=jnp.float32
    )


def first_dot(left, right):
    return lax.dot_general(
        left, right, (((0,), (0,)), ((), ())), preferred_element_type=jnp.float32
    )


def iota(shape, dim):
    return lax.broadcasted_iota(jnp.int32, shape, dim)


def as_bf16(mask):
    return mask.astype(jnp.float32).astype(jnp.bfloat16)


def as_column(row):
    count = row.shape[1]
    here = iota((count, count), 0) == iota((count, count), 1)
    return jnp.sum(jnp.where(here, row, 0.0), 1, keepdims=True)


def silu(value):
    return value / (1.0 + jnp.exp(-value))


SMEM = pl.BlockSpec(memory_space=pltpu.SMEM)
ANY = pl.BlockSpec(memory_space=pl.ANY)


def whole(array):
    return pl.BlockSpec(array.shape, lambda *_: (0,) * len(array.shape))


def in_hbm(array):
    return pltpu.with_memory_space_constraint(array, pltpu.HBM)


def in_vmem(array):
    return pltpu.with_memory_space_constraint(array, pltpu.VMEM)


def like(shape, dtype):
    return jax.ShapeDtypeStruct(shape, dtype)


def call(kernel, scalars, arrays, out_shape, flops=0, moved=1 << 20, unused=(), scratch=()):
    outs = out_shape if isinstance(out_shape, (list, tuple)) else [out_shape]
    count = len(scalars)

    def body(*refs):
        rest = refs[count + len(arrays) + len(unused) :]
        kernel(*refs[: count + len(arrays)], *rest)

    result = pl.pallas_call(
        body,
        out_shape=list(outs),
        in_specs=[SMEM] * count + [whole(a) for a in arrays] + [ANY] * len(unused),
        out_specs=[whole(o) for o in outs],
        scratch_shapes=list(scratch),
        compiler_params=pltpu.CompilerParams(vmem_limit_bytes=VMEM_LIMIT),
        cost_estimate=pl.CostEstimate(flops=flops, bytes_accessed=moved, transcendentals=0),
    )(*scalars, *arrays, *unused)
    return result if isinstance(out_shape, (list, tuple)) else result[0]


def attention_kernel(length, query, new_kv, cache, parents, attended):
    nodes = query.shape[1]
    heads = query.shape[2] // HD
    kv_heads = cache.shape[3] // HD
    group = heads // kv_heads
    shape = (nodes, nodes)
    parent = as_column(parents[...].astype(jnp.float32))
    column = iota(shape, 1).astype(jnp.float32)
    reach = ((column == parent) | (iota(shape, 0) == iota(shape, 1))).astype(jnp.float32)
    for _ in range(5):
        reach = jnp.minimum(dot32(reach.astype(jnp.bfloat16), reach.astype(jnp.bfloat16)), 1.0)
    reach = jnp.concatenate([reach] * group, 0)
    for kv in range(kv_heads):
        here = pl.ds(kv * HD, HD)
        first = kv * group
        rows = [query[0, :, (first + h) * HD : (first + h + 1) * HD] for h in range(group)]
        rows = jnp.concatenate(rows, 0)
        old = last_dot(rows, cache[0, 0, :, here]) * HD ** (-0.5)
        new = last_dot(rows, new_kv[0, 0, :, here]) * HD ** (-0.5)
        old = jnp.where(iota(old.shape, 1) < length[0], old, -jnp.inf)
        new = jnp.where(reach > 0.5, new, -jnp.inf)
        top = jnp.maximum(jnp.max(old, -1, keepdims=True), jnp.max(new, -1, keepdims=True))
        old, new = jnp.exp(old - top), jnp.exp(new - top)
        total = jnp.sum(old, -1, keepdims=True) + jnp.sum(new, -1, keepdims=True)
        mixed = dot32((old / total).astype(jnp.bfloat16), cache[1, 0, :, here])
        mixed = mixed + dot32((new / total).astype(jnp.bfloat16), new_kv[1, 0, :, here])
        mixed = mixed.astype(jnp.bfloat16)
        for h in range(group):
            attended[0, :, (first + h) * HD : (first + h + 1) * HD] = mixed[
                h * nodes : (h + 1) * nodes
            ]


def begin_kernel(accept, hidden, routes, gates, weights, bias, squares, notes, wide):
    rows = hidden[...].astype(jnp.float32)
    squares[...] = jnp.broadcast_to(jnp.sum(rows * rows, -1, keepdims=True), squares.shape)
    share = gates[...] / jnp.sum(gates[...], 0, keepdims=True)
    share_hi = share.astype(jnp.bfloat16).astype(jnp.float32)
    flag = (iota((TOPK, NODES), 1) == accept[0]).astype(jnp.float32)
    stack = [routes[...].astype(jnp.float32), share_hi, share - share_hi, flag]
    stack = jnp.concatenate(stack, 0).astype(jnp.bfloat16)
    places = as_bf16(iota((NODES, LANES), 0) == iota((NODES, LANES), 1))
    notes[...] = first_dot(stack, places).astype(jnp.bfloat16)
    block = weights.shape[1]
    lane = iota((block, LANES), 1)
    for head in range(2):
        wide[head, :, :D] = weights[head]
        value = as_column(bias[head : head + 1, :])
        extra = jnp.zeros((block, LANES), jnp.float32)
        for place in range(3):
            part = value.astype(jnp.bfloat16).astype(jnp.float32)
            extra = jnp.where(lane == place, part, extra)
            value = value - part
        wide[head, :, D:] = extra.astype(jnp.bfloat16)


def assemble_kernel(core, my_y, *refs):
    own, other, weights = refs[:NY], refs[NY], refs[NY + 1]
    block = own[0].shape[1]
    for step in range(NY):
        place = lax.rem(my_y[0] - step + NY, NY) * 2
        for head in range(2):
            here = pl.ds(pl.multiple_of((place + core[0]) * block, block), block)
            weights[head, here, :] = own[step][head]
            here = pl.ds(pl.multiple_of((place + 1 - core[0]) * block, block), block)
            weights[head, here, :] = other[step, head]


def pack_kernel(core, hidden, squares, gain, notes, packet):
    factor = lax.rsqrt(squares[...][:, :1] / D + eps_norm)
    own_gain = jnp.where(core[0] == 0, gain[:HALF], gain[HALF:]).reshape(1, HALF)
    normed = (hidden[...].astype(jnp.float32) * factor * own_gain).astype(jnp.bfloat16)
    for chip in range(NZ):
        packet[chip, :, :HALF] = normed
        packet[chip, :, HALF:] = notes[...]


def route_kernel(my_z, column, outgoing, mix_hi, mix_lo, accepted_mix):
    count = NZ * NODES
    slots = NZ * CAP
    tokens = column[...].reshape(count, HALF + LANES)
    turn = as_bf16(iota((NODES, LANES), 0) == iota((NODES, LANES), 1))
    notes = last_dot(turn, tokens[:, HALF:])
    expert = iota((NPLANE, 1), 0)
    expert = (((expert // 4) * NZ + my_z[0]) * 4 + expert % 4).astype(jnp.float32)
    member = jnp.zeros((NPLANE, count), jnp.float32)
    share_hi, share_lo = member, member
    for pick in range(TOPK):
        match = (notes[pick : pick + 1] == expert).astype(jnp.float32)
        member = member + match
        share_hi = share_hi + match * notes[TOPK + pick : TOPK + pick + 1]
        share_lo = share_lo + match * notes[2 * TOPK + pick : 2 * TOPK + pick + 1]
    first, second = iota((count, count), 0), iota((count, count), 1)
    earlier = (first < second) & (first // NODES == second // NODES)
    rank = dot32(member.astype(jnp.bfloat16), as_bf16(earlier))
    source = iota((1, count), 1) // NODES
    slot = jnp.where(member > 0.5, (source * CAP).astype(jnp.float32) + rank, -1.0)
    wanted = iota((slots, 1), 0).astype(jnp.float32)
    chosen = []
    for place in range(NPLANE):
        one = (slot[place : place + 1] == wanted).astype(jnp.float32)
        here = pl.ds(place * slots, slots)
        mix_hi[here, :] = (one * share_hi[place : place + 1]).astype(jnp.bfloat16)
        mix_lo[here, :] = (one * share_lo[place : place + 1]).astype(jnp.bfloat16)
        chosen.append(one.astype(jnp.bfloat16))
    chosen = jnp.concatenate(chosen, 0)
    for piece in range(HALF // BLOCK):
        here = slice(piece * BLOCK, (piece + 1) * BLOCK)
        part = dot32(chosen, tokens[:, here]).astype(jnp.bfloat16)
        outgoing[:, :, here] = part.reshape(NPLANE, slots, BLOCK)
    flag = notes[3 * TOPK : 3 * TOPK + 1]
    accepted = jnp.where(source == iota((NZ, 1), 0), flag, 0.0).astype(jnp.bfloat16)
    accepted_mix[:NZ] = last_dot(accepted, mix_hi[...]).astype(jnp.bfloat16)
    accepted_mix[NZ:] = last_dot(accepted, mix_lo[...]).astype(jnp.bfloat16)


def half_sums(core, rows, w_gate, w_up):
    here = pl.ds(pl.multiple_of(core * HALF, HALF), HALF)
    rows = rows[...].reshape(-1, HALF)
    return dot32(rows, w_gate[0, here, :]), dot32(rows, w_up[0, here, :])


def first_half_kernel(core, rows, w_gate, w_up, gate, up):
    gate[...], up[...] = half_sums(core[0], rows, w_gate, w_up)


def second_half_kernel(core, rows, w_gate, w_up, gate, up, activation):
    gate_part, up_part = half_sums(1 - core[0], rows, w_gate, w_up)
    activation[...] = (silu(gate[...] + gate_part) * (up[...] + up_part)).astype(jnp.bfloat16)


def down_kernel(core, own, other, down, other_down, finished):
    del core
    rows = jnp.concatenate([own[...], other[...]], 1)
    part = dot32(rows, jnp.concatenate([down[0], other_down[...]], 0))
    finished[...] = part.astype(jnp.bfloat16).reshape(finished.shape)


def down(core, own, other, w_down, other_down, out_shape):
    rows, units = own.shape
    steps = HALF // BLOCK
    column = lambda i, core: (0, i)
    return pl.pallas_call(
        down_kernel,
        out_shape=out_shape,
        grid_spec=pltpu.PrefetchScalarGridSpec(
            num_scalar_prefetch=1,
            grid=(steps,),
            in_specs=[
                pl.BlockSpec((rows, units), lambda i, core: (0, 0)),
                pl.BlockSpec((rows, units), lambda i, core: (0, 0)),
                pl.BlockSpec((1, units, BLOCK), lambda i, core: (0, 0, core[0] * steps + i)),
                pl.BlockSpec((units, BLOCK), column),
            ],
            out_specs=pl.BlockSpec((NPLANE, NZ * CAP, BLOCK), lambda i, core: (0, 0, i)),
        ),
        compiler_params=pltpu.CompilerParams(vmem_limit_bytes=VMEM_LIMIT),
        cost_estimate=pl.CostEstimate(
            flops=4 * rows * HALF * units, bytes_accessed=6 << 20, transcendentals=0
        ),
    )(core, own, other, w_down, other_down)


def combine_kernel(accept, my_z, mix, mix_hi, mix_lo, returned, hidden, parts, *refs):
    outs, partial = refs[:NZ], refs[NZ]
    rows = returned[...].reshape(-1, HALF)
    part = dot32(mix[...], rows)
    part = part[:NZ] + part[NZ:]
    here = iota((NODES, 1), 0) == accept[0]
    own = jnp.sum(jnp.where(here, hidden[...].astype(jnp.float32), 0.0), 0, keepdims=True)
    part = part + jnp.where(iota((NZ, 1), 0) == my_z[0], own, 0.0)
    quarter = HALF // 2
    for core in range(2):
        four = part[core * 4 : core * 4 + 4]
        four = jnp.concatenate([four[:, :quarter], four[:, quarter:]], 0).astype(jnp.bfloat16)
        for chip in range(NZ):
            parts[chip * 2 + core] = four
    partial[...] = first_dot(mix_hi[...], rows) + first_dot(mix_lo[...], rows)
    for step, out in enumerate(outs):
        place = lax.rem(my_z[0] + step, NZ)
        block = partial[pl.ds(pl.multiple_of(place * NODES, NODES), NODES), :]
        out[...] = block.astype(out.dtype)


def final_kernel(parts, gain, copies):
    quarter = parts.shape[2]
    chosen = jnp.sum(parts[...].reshape(NZ, 2, 8, quarter).astype(jnp.float32), 0)
    chosen = chosen.astype(jnp.bfloat16).astype(jnp.float32)
    squares = jnp.sum(jnp.sum(chosen * chosen, -1, keepdims=True), 0)
    squares = squares + jnp.concatenate([squares[4:], squares[:4]], 0)
    factor = lax.rsqrt(squares / D + eps_norm)
    first = iota((8, 1), 0) < 4
    for core in range(2):
        low = gain[core * HALF : core * HALF + quarter].reshape(1, quarter)
        high = gain[core * HALF + quarter : (core + 1) * HALF].reshape(1, quarter)
        final = (chosen[core] * factor * jnp.where(first, low, high)).astype(jnp.bfloat16)
        for chip in range(copies.shape[0]):
            copies[chip, core * 8 : (core + 1) * 8, :] = final


def medusa_kernel(tile, final, weights, copies):
    count, quarter = final.shape[0] * final.shape[1], final.shape[2]
    shape = (count // 4, count)
    row = iota(shape, 0)

    def pick(part):
        return as_bf16(iota(shape, 1) == row // 4 * 16 + part * 4 + row % 4)

    pieces = final[...].reshape(count, quarter)
    rows = [dot32(pick(part), pieces).astype(jnp.bfloat16) for part in range(4)]
    here = pl.ds(pl.multiple_of(tile[0] % NZ * LANES, LANES), LANES)
    own = dot32(pick(tile[0] // NZ), final[:, :, here].reshape(count, LANES))
    rows.append(as_bf16(iota((count // 4, LANES), 1) < 3))
    rows = jnp.concatenate(rows, 1)
    heads = [own + silu(last_dot(rows, weights[head])) for head in range(2)]
    heads = jnp.concatenate(heads, 0).astype(jnp.bfloat16)
    for chip in range(NZ):
        copies[chip] = heads


def copy_kernel(heads, copies):
    for chip in range(NPLANE):
        copies[chip] = heads[...]


def head_sums(heads, lm):
    tiles = []
    for x in range(4):
        for z in range(NZ):
            tiles.append(jnp.concatenate([heads[x * NY + y, z] for y in range(NY)], 0))
    return last_dot(lm[...], jnp.concatenate(tiles, 1))


def sums_kernel(heads, lm, total):
    total[...] = head_sums(heads, lm)


def logits_kernel(core, own, other, logits, stats):
    both = jnp.concatenate([own[...], other[...]], 1)
    shape = (2 * EXPERTS, 2 * EXPERTS)
    lane = iota(shape, 0)
    z = jnp.where(lane < EXPERTS, core[0], 1 - core[0]) * 4 + lane % 4
    wanted = lane // 16 % 2 * EXPERTS + lane // 4 % 4 * 32 + z * 4 + lane // 32 % 4
    order = as_bf16(wanted == iota(shape, 1))
    total = jnp.zeros(both.shape, jnp.float32)
    for _ in range(3):
        part = both.astype(jnp.bfloat16)
        total = total + dot32(part, order)
        both = both - part.astype(jnp.float32)
    top = jnp.max(total, 0, keepdims=True)
    sums = jnp.sum(jnp.exp(total - top), 0, keepdims=True)
    for head in range(2):
        here = slice(head * EXPERTS, (head + 1) * EXPERTS)
        logits[head] = total[:, here]
        for place in range(stats.shape[0]):
            stats[place, head : head + 1, :] = top[:, here]
            stats[place, 2 + head : 3 + head, :] = sums[:, here]


def merged(stats):
    tops, sums = stats[:, :2], stats[:, 2:]
    top = jnp.max(tops, 0)
    return top, jnp.sum(sums * jnp.exp(tops - top[None]), 0)


def merge_kernel(stats, copies):
    top, sums = merged(stats[...])
    for chip in range(NZ):
        copies[chip, :2, :] = top
        copies[chip, 2:, :] = sums


def finish_kernel(stats, logits, logprob):
    top, sums = merged(stats[...])
    shift = top + jnp.log(sums)
    for head in range(2):
        logprob[head] = logits[head] - shift[head : head + 1, :]


def on_device(
    query,
    new_kv,
    cache,
    cache_len,
    parents,
    hidden,
    moe_gain,
    routes,
    gates,
    w_gate,
    w_up,
    w_down,
    accept,
    final_gain,
    medusa_w,
    medusa_b,
    lm_head,
):
    bf16, f32 = jnp.bfloat16, jnp.float32
    core, my_z = lax.axis_index(TP), lax.axis_index("z")
    core_at, z_at, y_at = core.reshape(1), my_z.reshape(1), lax.axis_index("y").reshape(1)
    tile_at = (lax.axis_index("x") * NZ + my_z).reshape(1)
    slots = NPLANE * NZ * CAP
    units = w_gate.shape[2]
    vocab = lm_head.shape[0]

    squares, notes, wide_w = call(
        begin_kernel,
        [accept],
        [in_hbm(array) for array in (hidden, routes.T, gates.T, medusa_w, medusa_b)],
        [
            like((NODES, LANES), f32),
            like((NODES, LANES), bf16),
            like(medusa_w.shape[:2] + (D + LANES,), bf16),
        ],
    )

    packet = call(
        pack_kernel,
        [core_at],
        [in_hbm(hidden), lax.psum(squares, TP), in_hbm(moe_gain), notes],
        pltpu.HBM((NZ, NODES, HALF + LANES), bf16),
    )
    column = exchange(packet, "z")

    attended = call(
        attention_kernel,
        [cache_len],
        [query, new_kv, cache, parents],
        like(query.shape, bf16),
        flops=4 << 24,
        moved=4 << 20,
    )
    wide = [wide_w] + [lax.ppermute(wide_w, "y", around(NY, step)) for step in range(1, NY)]
    block_w = call(
        assemble_kernel,
        [core_at, y_at],
        wide + [swap(jnp.stack(wide))],
        pltpu.HBM((2, LANES, D + LANES), bf16),
        moved=4 << 20,
    )
    other_down = swap(lax.dynamic_slice_in_dim(w_down[0], (1 - core) * HALF, HALF, 1))

    other_lm = swap(lm_head)

    outgoing, mix_hi, mix_lo, accepted_mix = call(
        route_kernel,
        [z_at],
        [column],
        [
            pltpu.VMEM((NPLANE, NZ * CAP, HALF), bf16),
            pltpu.HBM((slots, NZ * NODES), bf16),
            pltpu.HBM((slots, NZ * NODES), bf16),
            like((2 * NZ, slots), bf16),
        ],
        flops=2 * slots * NZ * NODES * HALF,
        moved=4 << 20,
        unused=[in_hbm(attended), in_hbm(block_w), in_hbm(other_down), other_lm],
    )
    arrived = exchange(outgoing, PLANE)
    sums = call(
        first_half_kernel,
        [core_at],
        [arrived, w_gate, w_up],
        [like((slots, units), f32)] * 2,
        flops=4 * slots * HALF * units,
        moved=8 << 20,
    )
    activation = call(
        second_half_kernel,
        [core_at],
        [swap(arrived), w_gate, w_up, *sums],
        like((slots, units), bf16),
        flops=4 * slots * HALF * units,
        moved=8 << 20,
    )
    finished = down(
        core_at,
        activation,
        swap(activation),
        w_down,
        other_down,
        pltpu.VMEM((NPLANE, NZ * CAP, HALF), bf16),
    )
    returned = exchange(finished, PLANE)

    parts, own, *others = call(
        combine_kernel,
        [accept, z_at],
        [accepted_mix, in_hbm(mix_hi), in_hbm(mix_lo), returned, hidden],
        [pltpu.HBM((2 * NZ, NZ, HALF // 2), bf16), pltpu.HBM((NODES, HALF), f32)]
        + [pltpu.HBM((NODES, HALF), bf16)] * (NZ - 1),
        flops=4 * slots * NZ * NODES * HALF,
        moved=6 << 20,
        scratch=[pltpu.VMEM((NZ * NODES, HALF), f32)],
    )
    parts = exchange(parts, ("z", "c"))
    sent = {}
    for step, other in enumerate(others, 1):
        sent[step] = lax.ppermute(other, "z", around(NZ, step))

    final = call(
        final_kernel,
        [],
        [parts, in_hbm(final_gain)],
        pltpu.HBM((4, 16, HALF // 2), bf16),
        unused=[in_hbm(sent[1]), in_hbm(sent[7])],
    )
    final = exchange(final, "x")
    heads = call(
        medusa_kernel,
        [tile_at],
        [final, block_w],
        pltpu.HBM((NZ, 32, LANES), bf16),
        flops=2 * 16 * D * 256,
        moved=3 << 20,
    )
    heads = exchange(heads, "z")
    heads = call(
        copy_kernel,
        [],
        [heads],
        pltpu.VMEM((NPLANE, NZ, 32, LANES), bf16),
        unused=[in_hbm(sent[2]), in_hbm(sent[6])],
    )
    heads = exchange(heads, PLANE)
    to_other = call(
        sums_kernel,
        [],
        [heads, other_lm],
        like((vocab, EXPERTS), f32),
        flops=2 * EXPERTS * D * vocab,
        moved=4 << 20,
        unused=[in_hbm(sent[step]) for step in (3, 5, 4)],
    )
    to_own = call(
        sums_kernel,
        [],
        [heads, lm_head],
        like((vocab, EXPERTS), f32),
        flops=2 * EXPERTS * D * vocab,
        moved=4 << 20,
    )
    logits, stats = call(
        logits_kernel,
        [core_at],
        [to_own, swap(to_other)],
        [pltpu.HBM((2, vocab, EXPERTS), f32), pltpu.HBM((32, 4, EXPERTS), f32)],
        moved=1 << 20,
    )
    mixture = own
    for part in sent.values():
        mixture = mixture + part.astype(f32)
    layer_out = (hidden.astype(f32) + mixture).astype(bf16)
    stats = exchange(stats, ("x", "y", "c"))
    stats = call(merge_kernel, [], [stats], pltpu.HBM((NZ, 4, EXPERTS), f32))
    stats = exchange(stats, "z")
    logprob = call(finish_kernel, [], [stats, in_hbm(logits)], like((2, vocab, EXPERTS), f32))
    return (attended, layer_out, jnp.transpose(logprob, (0, 2, 1)))


def solution(mesh):
    fine = Mesh(mesh.devices.reshape(4, 8, 4, 2), ALL)
    in_specs = (
        P(EP, None, TP),
        P(None, EP, None, TP),
        P(None, EP, None, TP),
        P(EP),
        P(EP, None),
        P(EP, TP),
        P(),
        P(EP, None),
        P(EP, None),
        P(EP, None, TP),
        P(EP, None, TP),
        P(EP, TP, None),
        P(EP),
        P(),
        P(None, ALL, None),
        P(None, ALL),
        P(ALL, None),
    )
    out_specs = (P(EP, None, TP), P(EP, TP), P(None, None, ALL))
    return jax.shard_map(
        on_device, mesh=fine, in_specs=in_specs, out_specs=out_specs, check_vma=False
    )
```

```python
import jax
import jax.numpy as jnp
from jax import lax
from jax.experimental import pallas as pl
from jax.experimental.pallas import tpu as pltpu
from jax.sharding import Mesh, PartitionSpec as P

HD = 128
TOPK = 8
NODES = 32
CAP = 4
EXPERTS = 128
D = 4096
HALF = D // 2

eps_norm = 1e-06
EP = ("x", "z", "y")
TP = "c"
ALL = ("x", "z", "y", "c")
PLANE = ("x", "y")
NZ = 8
NY = 4
NPLANE = 16
LANES = 128
NEAR = (1, 2, -1, -2)
BLOCK = 512
VMEM_LIMIT = 40 << 20
SWAP = [(0, 1), (1, 0)]


def swap(value):
    return lax.ppermute(value, TP, SWAP)


def around(count, step):
    return [(chip, (chip + step) % count) for chip in range(count)]


def exchange(value, axes):
    return lax.all_to_all(value, axes, 0, 0, tiled=True)


def dot32(left, right):
    return jnp.dot(left, right, preferred_element_type=jnp.float32)


def last_dot(left, right):
    return lax.dot_general(
        left, right, (((1,), (1,)), ((), ())), preferred_element_type=jnp.float32
    )


def first_dot(left, right):
    return lax.dot_general(
        left, right, (((0,), (0,)), ((), ())), preferred_element_type=jnp.float32
    )


def iota(shape, dim):
    return lax.broadcasted_iota(jnp.int32, shape, dim)


def as_bf16(mask):
    return mask.astype(jnp.float32).astype(jnp.bfloat16)


def as_column(row):
    count = row.shape[1]
    here = iota((count, count), 0) == iota((count, count), 1)
    return jnp.sum(jnp.where(here, row, 0.0), 1, keepdims=True)


def silu(value):
    return value / (1.0 + jnp.exp(-value))


SMEM = pl.BlockSpec(memory_space=pltpu.SMEM)
ANY = pl.BlockSpec(memory_space=pl.ANY)


def whole(array):
    return pl.BlockSpec(array.shape, lambda *_: (0,) * len(array.shape))


def in_hbm(array):
    return pltpu.with_memory_space_constraint(array, pltpu.HBM)


def in_vmem(array):
    return pltpu.with_memory_space_constraint(array, pltpu.VMEM)


def like(shape, dtype):
    return jax.ShapeDtypeStruct(shape, dtype)


def call(kernel, scalars, arrays, out_shape, flops=0, moved=1 << 20, unused=(), scratch=()):
    outs = out_shape if isinstance(out_shape, (list, tuple)) else [out_shape]
    count = len(scalars)

    def body(*refs):
        rest = refs[count + len(arrays) + len(unused) :]
        kernel(*refs[: count + len(arrays)], *rest)

    result = pl.pallas_call(
        body,
        out_shape=list(outs),
        in_specs=[SMEM] * count + [whole(a) for a in arrays] + [ANY] * len(unused),
        out_specs=[whole(o) for o in outs],
        scratch_shapes=list(scratch),
        compiler_params=pltpu.CompilerParams(vmem_limit_bytes=VMEM_LIMIT),
        cost_estimate=pl.CostEstimate(flops=flops, bytes_accessed=moved, transcendentals=0),
    )(*scalars, *arrays, *unused)
    return result if isinstance(out_shape, (list, tuple)) else result[0]


def attention_kernel(length, query, new_kv, cache, parents, attended):
    nodes = query.shape[1]
    heads = query.shape[2] // HD
    kv_heads = cache.shape[3] // HD
    group = heads // kv_heads
    shape = (nodes, nodes)
    parent = as_column(parents[...].astype(jnp.float32))
    column = iota(shape, 1).astype(jnp.float32)
    reach = ((column == parent) | (iota(shape, 0) == iota(shape, 1))).astype(jnp.float32)
    for _ in range(5):
        reach = jnp.minimum(dot32(reach.astype(jnp.bfloat16), reach.astype(jnp.bfloat16)), 1.0)
    reach = jnp.concatenate([reach] * group, 0)
    for kv in range(kv_heads):
        here = pl.ds(kv * HD, HD)
        first = kv * group
        rows = [query[0, :, (first + h) * HD : (first + h + 1) * HD] for h in range(group)]
        rows = jnp.concatenate(rows, 0)
        old = last_dot(rows, cache[0, 0, :, here]) * HD ** (-0.5)
        new = last_dot(rows, new_kv[0, 0, :, here]) * HD ** (-0.5)
        old = jnp.where(iota(old.shape, 1) < length[0], old, -jnp.inf)
        new = jnp.where(reach > 0.5, new, -jnp.inf)
        top = jnp.maximum(jnp.max(old, -1, keepdims=True), jnp.max(new, -1, keepdims=True))
        old, new = jnp.exp(old - top), jnp.exp(new - top)
        total = jnp.sum(old, -1, keepdims=True) + jnp.sum(new, -1, keepdims=True)
        mixed = dot32((old / total).astype(jnp.bfloat16), cache[1, 0, :, here])
        mixed = mixed + dot32((new / total).astype(jnp.bfloat16), new_kv[1, 0, :, here])
        mixed = mixed.astype(jnp.bfloat16)
        for h in range(group):
            attended[0, :, (first + h) * HD : (first + h + 1) * HD] = mixed[
                h * nodes : (h + 1) * nodes
            ]


def begin_kernel(accept, hidden, routes, gates, squares, notes):
    rows = hidden[...].astype(jnp.float32)
    here = iota((NODES, LANES), 0) == iota((NODES, LANES), 1)
    sums = jnp.sum(rows * rows, -1, keepdims=True)
    squares[...] = jnp.sum(jnp.where(here, sums, 0.0), 0, keepdims=True)
    share = gates[...] / jnp.sum(gates[...], 0, keepdims=True)
    share_hi = share.astype(jnp.bfloat16).astype(jnp.float32)
    flag = (iota((TOPK, NODES), 1) == accept[0]).astype(jnp.float32)
    stack = [routes[...].astype(jnp.float32), share_hi, share - share_hi, flag]
    stack = jnp.concatenate(stack, 0).astype(jnp.bfloat16)
    notes[...] = first_dot(stack, as_bf16(here)).astype(jnp.bfloat16)


def widen_kernel(weights, bias, wide):
    block = weights.shape[1]
    lane = iota((block, LANES), 1)
    for head in range(2):
        wide[head, :, :D] = weights[head]
        value = as_column(bias[head : head + 1, :])
        extra = jnp.zeros((block, LANES), jnp.float32)
        for place in range(3):
            part = value.astype(jnp.bfloat16).astype(jnp.float32)
            extra = jnp.where(lane == place, part, extra)
            value = value - part
        wide[head, :, D:] = extra.astype(jnp.bfloat16)


def assemble_kernel(core, my_y, *refs):
    own, other, weights = refs[:NY], refs[NY], refs[NY + 1]
    block = own[0].shape[1]
    for step in range(NY):
        place = lax.rem(my_y[0] - step + NY, NY) * 2
        for head in range(2):
            here = pl.ds(pl.multiple_of((place + core[0]) * block, block), block)
            weights[head, here, :] = own[step][head]
            here = pl.ds(pl.multiple_of((place + 1 - core[0]) * block, block), block)
            weights[head, here, :] = other[step, head]


def pack_kernel(core, hidden, squares, gain, notes, packet):
    here = iota((NODES, LANES), 0) == iota((NODES, LANES), 1)
    sums = jnp.sum(jnp.where(here, squares[...], 0.0), 1, keepdims=True)
    factor = lax.rsqrt(sums / D + eps_norm)
    tiles = HALF // LANES
    for tile in range(tiles):
        own_gain = gain[pl.ds(core[0] * tiles + tile, 1), :]
        here = slice(tile * LANES, (tile + 1) * LANES)
        normed = hidden[:, here].astype(jnp.float32) * factor * own_gain
        normed = normed.astype(jnp.bfloat16)
        for chip in range(NZ):
            packet[chip, :, here] = normed
    for chip in range(NZ):
        packet[chip, :, HALF:] = notes[...]


def route_kernel(my_z, column, outgoing, mix_hi, mix_lo, accepted_mix):
    count = NZ * NODES
    slots = NZ * CAP
    tokens = column[...].reshape(count, HALF + LANES)
    turn = as_bf16(iota((NODES, LANES), 0) == iota((NODES, LANES), 1))
    notes = last_dot(turn, tokens[:, HALF:])
    expert = iota((NPLANE, 1), 0)
    expert = (((expert // 4) * NZ + my_z[0]) * 4 + expert % 4).astype(jnp.float32)
    member = jnp.zeros((NPLANE, count), jnp.float32)
    share_hi, share_lo = member, member
    for pick in range(TOPK):
        match = (notes[pick : pick + 1] == expert).astype(jnp.float32)
        member = member + match
        share_hi = share_hi + match * notes[TOPK + pick : TOPK + pick + 1]
        share_lo = share_lo + match * notes[2 * TOPK + pick : 2 * TOPK + pick + 1]
    first, second = iota((count, count), 0), iota((count, count), 1)
    earlier = (first < second) & (first // NODES == second // NODES)
    rank = dot32(member.astype(jnp.bfloat16), as_bf16(earlier))
    source = iota((1, count), 1) // NODES
    slot = jnp.where(member > 0.5, (source * CAP).astype(jnp.float32) + rank, -1.0)
    wanted = iota((slots, 1), 0).astype(jnp.float32)
    chosen = []
    for place in range(NPLANE):
        one = (slot[place : place + 1] == wanted).astype(jnp.float32)
        here = pl.ds(place * slots, slots)
        mix_hi[here, :] = (one * share_hi[place : place + 1]).astype(jnp.bfloat16)
        mix_lo[here, :] = (one * share_lo[place : place + 1]).astype(jnp.bfloat16)
        chosen.append(one.astype(jnp.bfloat16))
    chosen = jnp.concatenate(chosen, 0)
    for piece in range(HALF // BLOCK):
        here = slice(piece * BLOCK, (piece + 1) * BLOCK)
        part = dot32(chosen, tokens[:, here]).astype(jnp.bfloat16)
        outgoing[:, :, here] = part.reshape(NPLANE, slots, BLOCK)
    flag = notes[3 * TOPK : 3 * TOPK + 1]
    accepted = jnp.where(source == iota((NZ, 1), 0), flag, 0.0).astype(jnp.bfloat16)
    accepted_mix[:NZ] = last_dot(accepted, mix_hi[...]).astype(jnp.bfloat16)
    accepted_mix[NZ:] = last_dot(accepted, mix_lo[...]).astype(jnp.bfloat16)


def half_sums(core, rows, w_gate, w_up):
    here = pl.ds(pl.multiple_of(core * HALF, HALF), HALF)
    rows = rows[...].reshape(-1, HALF)
    return dot32(rows, w_gate[0, here, :]), dot32(rows, w_up[0, here, :])


def first_half_kernel(core, rows, w_gate, w_up, gate, up):
    gate[...], up[...] = half_sums(core[0], rows, w_gate, w_up)


def second_half_kernel(core, rows, w_gate, w_up, gate, up, activation):
    gate_part, up_part = half_sums(1 - core[0], rows, w_gate, w_up)
    activation[...] = (silu(gate[...] + gate_part) * (up[...] + up_part)).astype(jnp.bfloat16)


def down_kernel(core, own, other, down, other_down, finished):
    rows = jnp.concatenate([own[...], other[...]], 1)
    columns = pl.ds(pl.multiple_of(core[0] * HALF, HALF), HALF)
    weights = jnp.concatenate([down[0, :, columns], other_down[...]], 0)
    for piece in range(HALF // BLOCK):
        here = slice(piece * BLOCK, (piece + 1) * BLOCK)
        part = dot32(rows, weights[:, here]).astype(jnp.bfloat16)
        finished[:, :, here] = part.reshape(NPLANE, NZ * CAP, BLOCK)


def combine_kernel(
    accept, my_z, mix, mix_hi, mix_lo, returned, hidden, parts, own, far_up, far_down, near, total
):
    rows = returned[...].reshape(-1, HALF)
    part = dot32(mix[...], rows)
    part = part[:NZ] + part[NZ:]
    here = iota((NODES, 1), 0) == accept[0]
    row = jnp.sum(jnp.where(here, hidden[...].astype(jnp.float32), 0.0), 0, keepdims=True)
    part = part + jnp.where(iota((NZ, 1), 0) == my_z[0], row, 0.0)
    quarter = HALF // 2
    for core in range(2):
        four = part[core * 4 : core * 4 + 4]
        four = jnp.concatenate([four[:, :quarter], four[:, quarter:]], 0).astype(jnp.bfloat16)
        for chip in range(NZ):
            parts[chip * 2 + core] = four
    total[...] = first_dot(mix_hi[...], rows) + first_dot(mix_lo[...], rows)

    def block(step, first=0, count=NODES):
        place = lax.rem(my_z[0] + step + NZ, NZ)
        return total[pl.ds(pl.multiple_of(place * NODES + first, 16), count), :]

    own[...] = block(0)
    far_up[:NODES, :] = block(3).astype(jnp.bfloat16)
    far_up[NODES:, :] = block(4, 0, NODES // 2).astype(jnp.bfloat16)
    far_down[:NODES, :] = block(-3).astype(jnp.bfloat16)
    far_down[NODES:, :] = block(4, NODES // 2, NODES // 2).astype(jnp.bfloat16)
    for place, step in enumerate(NEAR):
        near[place] = block(step)


def relay_kernel(near, from_below, from_above, up1, up2, down1, down2):
    half = NODES // 2
    below, above = from_below[...].astype(jnp.float32), from_above[...].astype(jnp.float32)
    up1[...] = (near[0] + below[:NODES]).astype(jnp.bfloat16)
    up2[:half, :] = (near[1, :half] + below[NODES:]).astype(jnp.bfloat16)
    up2[half:, :] = near[1, half:].astype(jnp.bfloat16)
    down1[...] = (near[2] + above[:NODES]).astype(jnp.bfloat16)
    down2[:half, :] = near[3, :half].astype(jnp.bfloat16)
    down2[half:, :] = (near[3, half:] + above[NODES:]).astype(jnp.bfloat16)


def final_kernel(parts, gain, copies):
    quarter = parts.shape[2]
    chosen = jnp.sum(parts[...].reshape(NZ, 2, 8, quarter).astype(jnp.float32), 0)
    chosen = chosen.astype(jnp.bfloat16).astype(jnp.float32)
    squares = jnp.sum(jnp.sum(chosen * chosen, -1, keepdims=True), 0)
    squares = squares + jnp.concatenate([squares[4:], squares[:4]], 0)
    factor = lax.rsqrt(squares / D + eps_norm)
    first = iota((8, 1), 0) < 4
    tiles = quarter // LANES
    for core in range(2):
        for tile in range(tiles):
            low = core * 2 * tiles + tile
            own_gain = jnp.where(first, gain[low : low + 1], gain[low + tiles : low + tiles + 1])
            here = slice(tile * LANES, (tile + 1) * LANES)
            final = (chosen[core, :, here] * factor * own_gain).astype(jnp.bfloat16)
            for chip in range(copies.shape[0]):
                copies[chip, core * 8 : (core + 1) * 8, here] = final


def medusa_kernel(tile, final, weights, copies):
    count, quarter = final.shape[0] * final.shape[1], final.shape[2]
    shape = (count // 4, count)
    row = iota(shape, 0)

    def pick(part):
        return as_bf16(iota(shape, 1) == row // 4 * 16 + part * 4 + row % 4)

    pieces = final[...].reshape(count, quarter)
    rows = [dot32(pick(part), pieces).astype(jnp.bfloat16) for part in range(4)]
    here = pl.ds(pl.multiple_of(tile[0] % NZ * LANES, LANES), LANES)
    own = dot32(pick(tile[0] // NZ), final[:, :, here].reshape(count, LANES))
    rows.append(as_bf16(iota((count // 4, LANES), 1) < 3))
    rows = jnp.concatenate(rows, 1)
    heads = [own + silu(last_dot(rows, weights[head])) for head in range(2)]
    heads = jnp.concatenate(heads, 0).astype(jnp.bfloat16)
    for chip in range(NZ):
        copies[chip] = heads


def copy_kernel(heads, copies):
    for chip in range(NPLANE):
        copies[chip] = heads[...]


def head_sums(heads, lm):
    tiles = []
    for x in range(4):
        for z in range(NZ):
            tiles.append(jnp.concatenate([heads[x * NY + y, z] for y in range(NY)], 0))
    return last_dot(lm[...], jnp.concatenate(tiles, 1))


def sums_kernel(heads, lm, total):
    total[...] = head_sums(heads, lm)


def logits_kernel(core, own, other, logits, stats):
    both = jnp.concatenate([own[...], other[...]], 1)
    shape = (2 * EXPERTS, 2 * EXPERTS)
    lane = iota(shape, 0)
    z = jnp.where(lane < EXPERTS, core[0], 1 - core[0]) * 4 + lane % 4
    wanted = lane // 16 % 2 * EXPERTS + lane // 4 % 4 * 32 + z * 4 + lane // 32 % 4
    order = as_bf16(wanted == iota(shape, 1))
    total = jnp.zeros(both.shape, jnp.float32)
    for _ in range(3):
        part = both.astype(jnp.bfloat16)
        total = total + dot32(part, order)
        both = both - part.astype(jnp.float32)
    top = jnp.max(total, 0, keepdims=True)
    sums = jnp.sum(jnp.exp(total - top), 0, keepdims=True)
    for head in range(2):
        here = slice(head * EXPERTS, (head + 1) * EXPERTS)
        logits[head] = total[:, here]
        for place in range(stats.shape[0]):
            stats[place, head : head + 1, :] = top[:, here]
            stats[place, 2 + head : 3 + head, :] = sums[:, here]


def merged(stats):
    tops, sums = stats[:, :2], stats[:, 2:]
    top = jnp.max(tops, 0)
    return top, jnp.sum(sums * jnp.exp(tops - top[None]), 0)


def merge_kernel(stats, copies):
    top, sums = merged(stats[...])
    for chip in range(NZ):
        copies[chip, :2, :] = top
        copies[chip, 2:, :] = sums


def finish_kernel(stats, logits, logprob):
    top, sums = merged(stats[...])
    shift = top + jnp.log(sums)
    for head in range(2):
        logprob[head] = logits[head] - shift[head : head + 1, :]


def on_device(
    query,
    new_kv,
    cache,
    cache_len,
    parents,
    hidden,
    moe_gain,
    routes,
    gates,
    w_gate,
    w_up,
    w_down,
    accept,
    final_gain,
    medusa_w,
    medusa_b,
    lm_head,
):
    bf16, f32 = jnp.bfloat16, jnp.float32
    core, my_z = lax.axis_index(TP), lax.axis_index("z")
    core_at, z_at, y_at = core.reshape(1), my_z.reshape(1), lax.axis_index("y").reshape(1)
    tile_at = (lax.axis_index("x") * NZ + my_z).reshape(1)
    slots = NPLANE * NZ * CAP
    units = w_gate.shape[2]
    vocab = lm_head.shape[0]

    squares, notes = call(
        begin_kernel,
        [accept],
        [in_hbm(hidden), in_hbm(routes.T), in_hbm(gates.T)],
        [like((1, LANES), f32), like((NODES, LANES), bf16)],
    )

    packet = call(
        pack_kernel,
        [core_at],
        [in_hbm(hidden), lax.psum(squares, TP), in_hbm(moe_gain.reshape(-1, LANES)), notes],
        pltpu.HBM((NZ, NODES, HALF + LANES), bf16),
    )
    column = exchange(packet, "z")

    attended = call(
        attention_kernel,
        [cache_len],
        [query, new_kv, cache, parents],
        like(query.shape, bf16),
        flops=4 << 24,
        moved=4 << 20,
    )
    wide_w = call(
        widen_kernel,
        [],
        [in_hbm(medusa_w), in_hbm(medusa_b)],
        like(medusa_w.shape[:2] + (D + LANES,), bf16),
    )
    wide = [wide_w] + [lax.ppermute(wide_w, "y", around(NY, step)) for step in range(1, NY)]
    block_w = call(
        assemble_kernel,
        [core_at, y_at],
        wide + [swap(jnp.stack(wide))],
        pltpu.HBM((2, LANES, D + LANES), bf16),
        moved=4 << 20,
    )
    other_down = swap(lax.dynamic_slice_in_dim(w_down[0], (1 - core) * HALF, HALF, 1))

    other_lm = swap(lm_head)

    outgoing, mix_hi, mix_lo, accepted_mix = call(
        route_kernel,
        [z_at],
        [column],
        [
            pltpu.VMEM((NPLANE, NZ * CAP, HALF), bf16),
            pltpu.HBM((slots, NZ * NODES), bf16),
            pltpu.HBM((slots, NZ * NODES), bf16),
            like((2 * NZ, slots), bf16),
        ],
        flops=2 * slots * NZ * NODES * HALF,
        moved=4 << 20,
        unused=[in_hbm(attended), in_hbm(block_w), in_hbm(other_down), other_lm],
    )
    arrived = exchange(outgoing, PLANE)
    sums = call(
        first_half_kernel,
        [core_at],
        [arrived, w_gate, w_up],
        [like((slots, units), f32)] * 2,
        flops=4 * slots * HALF * units,
        moved=8 << 20,
    )
    activation = call(
        second_half_kernel,
        [core_at],
        [swap(arrived), w_gate, w_up, *sums],
        like((slots, units), bf16),
        flops=4 * slots * HALF * units,
        moved=8 << 20,
    )
    finished = call(
        down_kernel,
        [core_at],
        [activation, swap(activation), w_down, other_down],
        pltpu.VMEM((NPLANE, NZ * CAP, HALF), bf16),
        flops=4 * slots * HALF * units,
        moved=6 << 20,
    )
    returned = exchange(finished, PLANE)

    parts, own, far_up, far_down, near = call(
        combine_kernel,
        [accept, z_at],
        [accepted_mix, in_hbm(mix_hi), in_hbm(mix_lo), returned, hidden],
        [
            pltpu.HBM((2 * NZ, NZ, HALF // 2), bf16),
            pltpu.HBM((NODES, HALF), f32),
            pltpu.HBM((NODES * 3 // 2, HALF), bf16),
            pltpu.HBM((NODES * 3 // 2, HALF), bf16),
            pltpu.HBM((len(NEAR), NODES, HALF), f32),
        ],
        flops=4 * slots * NZ * NODES * HALF,
        moved=6 << 20,
        scratch=[pltpu.VMEM((NZ * NODES, HALF), f32)],
    )
    parts = exchange(parts, ("z", "c"))
    from_below = in_hbm(lax.ppermute(far_up, "z", around(NZ, 2)))
    from_above = in_hbm(lax.ppermute(far_down, "z", around(NZ, -2)))
    relayed = call(
        relay_kernel,
        [],
        [in_hbm(near), from_below, from_above],
        [pltpu.HBM((NODES, HALF), bf16)] * len(NEAR),
        moved=2 << 20,
    )
    sent = [
        lax.ppermute(part, "z", around(NZ, step)) for step, part in zip(NEAR, relayed)
    ]

    final = call(
        final_kernel,
        [],
        [parts, in_hbm(final_gain.reshape(-1, LANES))],
        pltpu.HBM((4, 16, HALF // 2), bf16),
    )
    final = exchange(final, "x")
    heads = call(
        medusa_kernel,
        [tile_at],
        [final, block_w],
        pltpu.HBM((NZ, 32, LANES), bf16),
        flops=2 * 16 * D * 256,
        moved=3 << 20,
    )
    heads = exchange(heads, "z")
    heads = call(
        copy_kernel,
        [],
        [heads],
        pltpu.HBM((NPLANE, NZ, 32, LANES), bf16),
        unused=[from_below, from_above],
    )
    heads = exchange(heads, PLANE)
    to_other = call(
        sums_kernel,
        [],
        [heads, other_lm],
        like((vocab, EXPERTS), f32),
        flops=2 * EXPERTS * D * vocab,
        moved=4 << 20,
        unused=[in_hbm(part) for part in sent],
    )
    to_own = call(
        sums_kernel,
        [],
        [heads, lm_head],
        like((vocab, EXPERTS), f32),
        flops=2 * EXPERTS * D * vocab,
        moved=4 << 20,
    )
    logits, stats = call(
        logits_kernel,
        [core_at],
        [to_own, swap(to_other)],
        [pltpu.HBM((2, vocab, EXPERTS), f32), pltpu.HBM((32, 4, EXPERTS), f32)],
        moved=1 << 20,
    )
    mixture = own
    for part in sent:
        mixture = mixture + part.astype(f32)
    layer_out = (hidden.astype(f32) + mixture).astype(bf16)
    stats = exchange(stats, ("x", "y", "c"))
    stats = call(merge_kernel, [], [stats], pltpu.HBM((NZ, 4, EXPERTS), f32))
    stats = exchange(stats, "z")
    logprob = call(finish_kernel, [], [stats, in_hbm(logits)], like((2, vocab, EXPERTS), f32))
    return (attended, layer_out, jnp.transpose(logprob, (0, 2, 1)))


def solution(mesh):
    fine = Mesh(mesh.devices.reshape(4, 8, 4, 2), ALL)
    in_specs = (
        P(EP, None, TP),
        P(None, EP, None, TP),
        P(None, EP, None, TP),
        P(EP),
        P(EP, None),
        P(EP, TP),
        P(),
        P(EP, None),
        P(EP, None),
        P(EP, None, TP),
        P(EP, None, TP),
        P(EP, TP, None),
        P(EP),
        P(),
        P(None, ALL, None),
        P(None, ALL),
        P(ALL, None),
    )
    out_specs = (P(EP, None, TP), P(EP, TP), P(None, None, ALL))
    return jax.shard_map(
        on_device, mesh=fine, in_specs=in_specs, out_specs=out_specs, check_vma=False
    )
```

```python
import jax
import jax.numpy as jnp
from jax import lax
from jax.experimental import pallas as pl
from jax.experimental.pallas import tpu as pltpu
from jax.sharding import Mesh, PartitionSpec as P

HD = 128
TOPK = 8
NODES = 32
CAP = 4
EXPERTS = 128
D = 4096
HALF = D // 2

eps_norm = 1e-06
EP = ("x", "z", "y")
TP = "c"
ALL = ("x", "z", "y", "c")
PLANE = ("x", "y")
NZ = 8
NY = 4
NPLANE = 16
LANES = 128
NEAR = (1, 2, -1, -2)
BLOCK = 512
VMEM_LIMIT = 24 << 20
SWAP = [(0, 1), (1, 0)]


def swap(value):
    return lax.ppermute(value, TP, SWAP)


def around(count, step):
    return [(chip, (chip + step) % count) for chip in range(count)]


def exchange(value, axes):
    return lax.all_to_all(value, axes, 0, 0, tiled=True)


def dot32(left, right):
    return jnp.dot(left, right, preferred_element_type=jnp.float32)


def last_dot(left, right):
    return lax.dot_general(
        left, right, (((1,), (1,)), ((), ())), preferred_element_type=jnp.float32
    )


def first_dot(left, right):
    return lax.dot_general(
        left, right, (((0,), (0,)), ((), ())), preferred_element_type=jnp.float32
    )


def iota(shape, dim):
    return lax.broadcasted_iota(jnp.int32, shape, dim)


def as_bf16(mask):
    return mask.astype(jnp.float32).astype(jnp.bfloat16)


def as_column(row):
    count = row.shape[1]
    here = iota((count, count), 0) == iota((count, count), 1)
    return jnp.sum(jnp.where(here, row, 0.0), 1, keepdims=True)


def silu(value):
    return value / (1.0 + jnp.exp(-value))


SMEM = pl.BlockSpec(memory_space=pltpu.SMEM)
ANY = pl.BlockSpec(memory_space=pl.ANY)


def whole(array):
    return pl.BlockSpec(array.shape, lambda *_: (0,) * len(array.shape))


def in_hbm(array):
    return pltpu.with_memory_space_constraint(array, pltpu.HBM)


def in_vmem(array):
    return pltpu.with_memory_space_constraint(array, pltpu.VMEM)


def like(shape, dtype):
    return jax.ShapeDtypeStruct(shape, dtype)


def call(kernel, scalars, arrays, out_shape, flops=0, moved=1 << 20, unused=(), scratch=()):
    outs = out_shape if isinstance(out_shape, (list, tuple)) else [out_shape]
    count = len(scalars)

    def body(*refs):
        rest = refs[count + len(arrays) + len(unused) :]
        kernel(*refs[: count + len(arrays)], *rest)

    result = pl.pallas_call(
        body,
        out_shape=list(outs),
        in_specs=[SMEM] * count + [whole(a) for a in arrays] + [ANY] * len(unused),
        out_specs=[whole(o) for o in outs],
        scratch_shapes=list(scratch),
        compiler_params=pltpu.CompilerParams(vmem_limit_bytes=VMEM_LIMIT),
        cost_estimate=pl.CostEstimate(flops=flops, bytes_accessed=moved, transcendentals=0),
    )(*scalars, *arrays, *unused)
    return result if isinstance(out_shape, (list, tuple)) else result[0]


def attention_kernel(length, query, new_kv, cache, parents, attended):
    nodes = query.shape[1]
    heads = query.shape[2] // HD
    kv_heads = cache.shape[3] // HD
    group = heads // kv_heads
    shape = (nodes, nodes)
    parent = as_column(parents[...].astype(jnp.float32))
    column = iota(shape, 1).astype(jnp.float32)
    reach = ((column == parent) | (iota(shape, 0) == iota(shape, 1))).astype(jnp.float32)
    for _ in range(5):
        reach = jnp.minimum(dot32(reach.astype(jnp.bfloat16), reach.astype(jnp.bfloat16)), 1.0)
    reach = jnp.concatenate([reach] * group, 0)
    for kv in range(kv_heads):
        here = pl.ds(kv * HD, HD)
        first = kv * group
        rows = [query[0, :, (first + h) * HD : (first + h + 1) * HD] for h in range(group)]
        rows = jnp.concatenate(rows, 0)
        old = last_dot(rows, cache[0, 0, :, here]) * HD ** (-0.5)
        new = last_dot(rows, new_kv[0, 0, :, here]) * HD ** (-0.5)
        old = jnp.where(iota(old.shape, 1) < length[0], old, -jnp.inf)
        new = jnp.where(reach > 0.5, new, -jnp.inf)
        top = jnp.maximum(jnp.max(old, -1, keepdims=True), jnp.max(new, -1, keepdims=True))
        old, new = jnp.exp(old - top), jnp.exp(new - top)
        total = jnp.sum(old, -1, keepdims=True) + jnp.sum(new, -1, keepdims=True)
        mixed = dot32((old / total).astype(jnp.bfloat16), cache[1, 0, :, here])
        mixed = mixed + dot32((new / total).astype(jnp.bfloat16), new_kv[1, 0, :, here])
        mixed = mixed.astype(jnp.bfloat16)
        for h in range(group):
            attended[0, :, (first + h) * HD : (first + h + 1) * HD] = mixed[
                h * nodes : (h + 1) * nodes
            ]


def begin_kernel(accept, hidden, routes, gates, packet):
    share = gates[...] / jnp.sum(gates[...], 0, keepdims=True)
    share_hi = share.astype(jnp.bfloat16).astype(jnp.float32)
    flag = (iota((TOPK, NODES), 1) == accept[0]).astype(jnp.float32)
    stack = [routes[...].astype(jnp.float32), share_hi, share - share_hi, flag]
    stack = jnp.concatenate(stack, 0).astype(jnp.bfloat16)
    here = iota((NODES, LANES), 0) == iota((NODES, LANES), 1)
    notes = first_dot(stack, as_bf16(here)).astype(jnp.bfloat16)
    for chip in range(NZ):
        packet[chip, :, :HALF] = hidden[...]
        packet[chip, :, HALF:] = notes


def widen_kernel(weights, bias, wide):
    block = weights.shape[1]
    lane = iota((block, LANES), 1)
    for head in range(2):
        wide[head, :, :D] = weights[head]
        value = as_column(bias[head : head + 1, :])
        extra = jnp.zeros((block, LANES), jnp.float32)
        for place in range(3):
            part = value.astype(jnp.bfloat16).astype(jnp.float32)
            extra = jnp.where(lane == place, part, extra)
            value = value - part
        wide[head, :, D:] = extra.astype(jnp.bfloat16)


def assemble_kernel(core, my_y, *refs):
    own, other, weights = refs[:NY], refs[NY], refs[NY + 1]
    block = own[0].shape[1]
    for step in range(NY):
        place = lax.rem(my_y[0] - step + NY, NY) * 2
        for head in range(2):
            here = pl.ds(pl.multiple_of((place + core[0]) * block, block), block)
            weights[head, here, :] = own[step][head]
            here = pl.ds(pl.multiple_of((place + 1 - core[0]) * block, block), block)
            weights[head, here, :] = other[step, head]


def route_kernel(my_z, column, outgoing, mix_hi, mix_lo, accepted_mix):
    count = NZ * NODES
    slots = NZ * CAP
    tokens = column[...].reshape(count, HALF + LANES)
    turn = as_bf16(iota((NODES, LANES), 0) == iota((NODES, LANES), 1))
    notes = last_dot(turn, tokens[:, HALF:])
    expert = iota((NPLANE, 1), 0)
    expert = (((expert // 4) * NZ + my_z[0]) * 4 + expert % 4).astype(jnp.float32)
    member = jnp.zeros((NPLANE, count), jnp.float32)
    share_hi, share_lo = member, member
    for pick in range(TOPK):
        match = (notes[pick : pick + 1] == expert).astype(jnp.float32)
        member = member + match
        share_hi = share_hi + match * notes[TOPK + pick : TOPK + pick + 1]
        share_lo = share_lo + match * notes[2 * TOPK + pick : 2 * TOPK + pick + 1]
    first, second = iota((count, count), 0), iota((count, count), 1)
    earlier = (first < second) & (first // NODES == second // NODES)
    rank = dot32(member.astype(jnp.bfloat16), as_bf16(earlier))
    source = iota((1, count), 1) // NODES
    slot = jnp.where(member > 0.5, (source * CAP).astype(jnp.float32) + rank, -1.0)
    wanted = iota((slots, 1), 0).astype(jnp.float32)
    chosen = []
    for place in range(NPLANE):
        one = (slot[place : place + 1] == wanted).astype(jnp.float32)
        here = pl.ds(place * slots, slots)
        mix_hi[here, :] = (one * share_hi[place : place + 1]).astype(jnp.bfloat16)
        mix_lo[here, :] = (one * share_lo[place : place + 1]).astype(jnp.bfloat16)
        chosen.append(one.astype(jnp.bfloat16))
    chosen = jnp.concatenate(chosen, 0)
    for piece in range(HALF // BLOCK):
        here = slice(piece * BLOCK, (piece + 1) * BLOCK)
        part = dot32(chosen, tokens[:, here]).astype(jnp.bfloat16)
        outgoing[:, :, here] = part.reshape(NPLANE, slots, BLOCK)
    flag = notes[3 * TOPK : 3 * TOPK + 1]
    accepted = jnp.where(source == iota((NZ, 1), 0), flag, 0.0).astype(jnp.bfloat16)
    accepted_mix[:NZ] = last_dot(accepted, mix_hi[...]).astype(jnp.bfloat16)
    accepted_mix[NZ:] = last_dot(accepted, mix_lo[...]).astype(jnp.bfloat16)


def squares_kernel(arrived, squares):
    count = squares.shape[0] * LANES
    total = jnp.zeros((count, LANES), jnp.float32)
    for tile in range(HALF // LANES):
        here = slice(tile * LANES, (tile + 1) * LANES)
        values = arrived[:, :, here].reshape(count, LANES).astype(jnp.float32)
        total = total + values * values
    total = jnp.sum(total, -1, keepdims=True)
    here = iota((LANES, LANES), 0) == iota((LANES, LANES), 1)
    for place in range(squares.shape[0]):
        part = total[place * LANES : (place + 1) * LANES]
        squares[place : place + 1, :] = jnp.sum(jnp.where(here, part, 0.0), 0, keepdims=True)


def half_sums(core, arrived, own, other, gain, w_gate, w_up, rows):
    count = rows.shape[0]
    tiles = HALF // LANES
    sums = own[...] + other[...]
    sums = [as_column(sums[place : place + 1, :]) for place in range(count // LANES)]
    factor = lax.rsqrt(jnp.concatenate(sums, 0) / D + eps_norm)
    for tile in range(tiles):
        here = slice(tile * LANES, (tile + 1) * LANES)
        values = arrived[:, :, here].reshape(count, LANES).astype(jnp.float32)
        values = values * factor * gain[pl.ds(core * tiles + tile, 1), :]
        rows[:, here] = values.astype(jnp.bfloat16)
    here = pl.ds(pl.multiple_of(core * HALF, HALF), HALF)
    return dot32(rows[...], w_gate[0, here, :]), dot32(rows[...], w_up[0, here, :])


def first_half_kernel(core, arrived, own, other, gain, w_gate, w_up, gate, up, rows):
    gate[...], up[...] = half_sums(core[0], arrived, own, other, gain, w_gate, w_up, rows)


def second_half_kernel(
    core, arrived, own, other, gain, w_gate, w_up, gate, up, activation, rows
):
    gate_part, up_part = half_sums(1 - core[0], arrived, own, other, gain, w_gate, w_up, rows)
    activation[...] = (silu(gate[...] + gate_part) * (up[...] + up_part)).astype(jnp.bfloat16)


def down_kernel(core, own, other, down, other_down, finished):
    rows = jnp.concatenate([own[...], other[...]], 1)
    columns = pl.ds(pl.multiple_of(core[0] * HALF, HALF), HALF)
    weights = jnp.concatenate([down[0, :, columns], other_down[...]], 0)
    for piece in range(HALF // BLOCK):
        here = slice(piece * BLOCK, (piece + 1) * BLOCK)
        part = dot32(rows, weights[:, here]).astype(jnp.bfloat16)
        finished[:, :, here] = part.reshape(NPLANE, NZ * CAP, BLOCK)


def combine_kernel(
    accept, my_z, mix, mix_hi, mix_lo, returned, hidden, parts, own, far_up, far_down, near, total
):
    rows = returned[...].reshape(-1, HALF)
    part = dot32(mix[...], rows)
    part = part[:NZ] + part[NZ:]
    here = iota((NODES, 1), 0) == accept[0]
    row = jnp.sum(jnp.where(here, hidden[...].astype(jnp.float32), 0.0), 0, keepdims=True)
    part = part + jnp.where(iota((NZ, 1), 0) == my_z[0], row, 0.0)
    quarter = HALF // 2
    for core in range(2):
        four = part[core * 4 : core * 4 + 4]
        four = jnp.concatenate([four[:, :quarter], four[:, quarter:]], 0).astype(jnp.bfloat16)
        for chip in range(NZ):
            parts[chip * 2 + core] = four
    total[...] = first_dot(mix_hi[...], rows) + first_dot(mix_lo[...], rows)

    def block(step, first=0, count=NODES):
        place = lax.rem(my_z[0] + step + NZ, NZ)
        return total[pl.ds(pl.multiple_of(place * NODES + first, 16), count), :]

    own[...] = block(0)
    far_up[:NODES, :] = block(3).astype(jnp.bfloat16)
    far_up[NODES:, :] = block(4, 0, NODES // 2).astype(jnp.bfloat16)
    far_down[:NODES, :] = block(-3).astype(jnp.bfloat16)
    far_down[NODES:, :] = block(4, NODES // 2, NODES // 2).astype(jnp.bfloat16)
    for place, step in enumerate(NEAR):
        near[place] = block(step)


def relay_kernel(near, from_below, from_above, up1, up2, down1, down2):
    half = NODES // 2
    below, above = from_below[...].astype(jnp.float32), from_above[...].astype(jnp.float32)
    up1[...] = (near[0] + below[:NODES]).astype(jnp.bfloat16)
    up2[:half, :] = (near[1, :half] + below[NODES:]).astype(jnp.bfloat16)
    up2[half:, :] = near[1, half:].astype(jnp.bfloat16)
    down1[...] = (near[2] + above[:NODES]).astype(jnp.bfloat16)
    down2[:half, :] = near[3, :half].astype(jnp.bfloat16)
    down2[half:, :] = (near[3, half:] + above[NODES:]).astype(jnp.bfloat16)


def final_kernel(parts, gain, copies):
    quarter = parts.shape[2]
    chosen = jnp.sum(parts[...].reshape(NZ, 2, 8, quarter).astype(jnp.float32), 0)
    chosen = chosen.astype(jnp.bfloat16).astype(jnp.float32)
    squares = jnp.sum(jnp.sum(chosen * chosen, -1, keepdims=True), 0)
    squares = squares + jnp.concatenate([squares[4:], squares[:4]], 0)
    factor = lax.rsqrt(squares / D + eps_norm)
    first = iota((8, 1), 0) < 4
    tiles = quarter // LANES
    for core in range(2):
        for tile in range(tiles):
            low = core * 2 * tiles + tile
            own_gain = jnp.where(first, gain[low : low + 1], gain[low + tiles : low + tiles + 1])
            here = slice(tile * LANES, (tile + 1) * LANES)
            final = (chosen[core, :, here] * factor * own_gain).astype(jnp.bfloat16)
            for chip in range(copies.shape[0]):
                copies[chip, core * 8 : (core + 1) * 8, here] = final


def medusa_kernel(tile, final, weights, copies):
    count, quarter = final.shape[0] * final.shape[1], final.shape[2]
    shape = (count // 4, count)
    row = iota(shape, 0)

    def pick(part):
        return as_bf16(iota(shape, 1) == row // 4 * 16 + part * 4 + row % 4)

    pieces = final[...].reshape(count, quarter)
    rows = [dot32(pick(part), pieces).astype(jnp.bfloat16) for part in range(4)]
    here = pl.ds(pl.multiple_of(tile[0] % NZ * LANES, LANES), LANES)
    own = dot32(pick(tile[0] // NZ), final[:, :, here].reshape(count, LANES))
    rows.append(as_bf16(iota((count // 4, LANES), 1) < 3))
    rows = jnp.concatenate(rows, 1)
    heads = [own + silu(last_dot(rows, weights[head])) for head in range(2)]
    heads = jnp.concatenate(heads, 0).astype(jnp.bfloat16)
    for chip in range(NZ):
        copies[chip] = heads


def copy_kernel(heads, copies):
    for chip in range(NPLANE):
        copies[chip] = heads[...]


def head_sums(heads, lm):
    tiles = []
    for x in range(4):
        for z in range(NZ):
            tiles.append(jnp.concatenate([heads[x * NY + y, z] for y in range(NY)], 0))
    return last_dot(lm[...], jnp.concatenate(tiles, 1))


def sums_kernel(heads, lm, total):
    total[...] = head_sums(heads, lm)


def logits_kernel(core, own, other, logits, stats):
    both = jnp.concatenate([own[...], other[...]], 1)
    shape = (2 * EXPERTS, 2 * EXPERTS)
    lane = iota(shape, 0)
    z = jnp.where(lane < EXPERTS, core[0], 1 - core[0]) * 4 + lane % 4
    wanted = lane // 16 % 2 * EXPERTS + lane // 4 % 4 * 32 + z * 4 + lane // 32 % 4
    order = as_bf16(wanted == iota(shape, 1))
    total = jnp.zeros(both.shape, jnp.float32)
    for _ in range(3):
        part = both.astype(jnp.bfloat16)
        total = total + dot32(part, order)
        both = both - part.astype(jnp.float32)
    top = jnp.max(total, 0, keepdims=True)
    sums = jnp.sum(jnp.exp(total - top), 0, keepdims=True)
    for head in range(2):
        here = slice(head * EXPERTS, (head + 1) * EXPERTS)
        logits[head] = total[:, here]
        for place in range(stats.shape[0]):
            stats[place, head : head + 1, :] = top[:, here]
            stats[place, 2 + head : 3 + head, :] = sums[:, here]


def merged(stats):
    tops, sums = stats[:, :2], stats[:, 2:]
    top = jnp.max(tops, 0)
    return top, jnp.sum(sums * jnp.exp(tops - top[None]), 0)


def merge_kernel(stats, copies):
    top, sums = merged(stats[...])
    for chip in range(NZ):
        copies[chip, :2, :] = top
        copies[chip, 2:, :] = sums


def finish_kernel(stats, logits, logprob):
    top, sums = merged(stats[...])
    shift = top + jnp.log(sums)
    for head in range(2):
        logprob[head] = logits[head] - shift[head : head + 1, :]


def on_device(
    query,
    new_kv,
    cache,
    cache_len,
    parents,
    hidden,
    moe_gain,
    routes,
    gates,
    w_gate,
    w_up,
    w_down,
    accept,
    final_gain,
    medusa_w,
    medusa_b,
    lm_head,
):
    bf16, f32 = jnp.bfloat16, jnp.float32
    core, my_z = lax.axis_index(TP), lax.axis_index("z")
    core_at, z_at, y_at = core.reshape(1), my_z.reshape(1), lax.axis_index("y").reshape(1)
    tile_at = (lax.axis_index("x") * NZ + my_z).reshape(1)
    slots = NPLANE * NZ * CAP
    units = w_gate.shape[2]
    vocab = lm_head.shape[0]

    packet = call(
        begin_kernel,
        [accept],
        [in_hbm(hidden), in_hbm(routes.T), in_hbm(gates.T)],
        pltpu.HBM((NZ, NODES, HALF + LANES), bf16),
    )
    column = exchange(packet, "z")

    attended = call(
        attention_kernel,
        [cache_len],
        [query, new_kv, cache, parents],
        like(query.shape, bf16),
        flops=4 << 24,
        moved=4 << 20,
    )
    wide_w = call(
        widen_kernel,
        [],
        [in_hbm(medusa_w), in_hbm(medusa_b)],
        like(medusa_w.shape[:2] + (D + LANES,), bf16),
    )
    wide = [wide_w] + [lax.ppermute(wide_w, "y", around(NY, step)) for step in range(1, NY)]
    block_w = call(
        assemble_kernel,
        [core_at, y_at],
        wide + [swap(jnp.stack(wide))],
        pltpu.HBM((2, LANES, D + LANES), bf16),
        moved=4 << 20,
    )
    other_down = swap(lax.dynamic_slice_in_dim(w_down[0], (1 - core) * HALF, HALF, 1))

    other_lm = swap(lm_head)

    outgoing, mix_hi, mix_lo, accepted_mix = call(
        route_kernel,
        [z_at],
        [column],
        [
            pltpu.VMEM((NPLANE, NZ * CAP, HALF), bf16),
            pltpu.HBM((slots, NZ * NODES), bf16),
            pltpu.HBM((slots, NZ * NODES), bf16),
            like((2 * NZ, slots), bf16),
        ],
        flops=2 * slots * NZ * NODES * HALF,
        moved=4 << 20,
        unused=[in_hbm(attended), in_hbm(block_w), in_hbm(other_down), other_lm],
    )
    arrived = exchange(outgoing, PLANE)
    squares = call(squares_kernel, [], [arrived], like((slots // LANES, LANES), f32))
    both = [squares, swap(squares)]
    gain = moe_gain.reshape(-1, LANES)
    sums = call(
        first_half_kernel,
        [core_at],
        [arrived, *both, gain, w_gate, w_up],
        [like((slots, units), f32)] * 2,
        flops=4 * slots * HALF * units,
        moved=8 << 20,
        scratch=[pltpu.VMEM((slots, HALF), bf16)],
    )
    activation = call(
        second_half_kernel,
        [core_at],
        [swap(arrived), *both, gain, w_gate, w_up, *sums],
        like((slots, units), bf16),
        flops=4 * slots * HALF * units,
        moved=8 << 20,
        scratch=[pltpu.VMEM((slots, HALF), bf16)],
    )
    finished = call(
        down_kernel,
        [core_at],
        [activation, swap(activation), w_down, other_down],
        pltpu.VMEM((NPLANE, NZ * CAP, HALF), bf16),
        flops=4 * slots * HALF * units,
        moved=6 << 20,
    )
    returned = exchange(finished, PLANE)

    parts, own, far_up, far_down, near = call(
        combine_kernel,
        [accept, z_at],
        [accepted_mix, in_hbm(mix_hi), in_hbm(mix_lo), returned, hidden],
        [
            pltpu.HBM((2 * NZ, NZ, HALF // 2), bf16),
            pltpu.HBM((NODES, HALF), f32),
            pltpu.HBM((NODES * 3 // 2, HALF), bf16),
            pltpu.HBM((NODES * 3 // 2, HALF), bf16),
            pltpu.HBM((len(NEAR), NODES, HALF), f32),
        ],
        flops=4 * slots * NZ * NODES * HALF,
        moved=6 << 20,
        scratch=[pltpu.VMEM((NZ * NODES, HALF), f32)],
    )
    parts = exchange(parts, ("z", "c"))
    from_below = in_hbm(lax.ppermute(far_up, "z", around(NZ, 2)))
    from_above = in_hbm(lax.ppermute(far_down, "z", around(NZ, -2)))
    relayed = call(
        relay_kernel,
        [],
        [in_hbm(near), from_below, from_above],
        [pltpu.HBM((NODES, HALF), bf16)] * len(NEAR),
        moved=2 << 20,
    )
    sent = [
        lax.ppermute(part, "z", around(NZ, step)) for step, part in zip(NEAR, relayed)
    ]

    final = call(
        final_kernel,
        [],
        [parts, in_hbm(final_gain.reshape(-1, LANES))],
        pltpu.HBM((4, 16, HALF // 2), bf16),
    )
    final = exchange(final, "x")
    heads = call(
        medusa_kernel,
        [tile_at],
        [final, block_w],
        pltpu.HBM((NZ, 32, LANES), bf16),
        flops=2 * 16 * D * 256,
        moved=3 << 20,
    )
    heads = exchange(heads, "z")
    heads = call(
        copy_kernel,
        [],
        [heads],
        pltpu.HBM((NPLANE, NZ, 32, LANES), bf16),
        unused=[in_hbm(relayed[0])],
    )
    heads = exchange(heads, PLANE)
    to_other = call(
        sums_kernel,
        [],
        [heads, other_lm],
        like((vocab, EXPERTS), f32),
        flops=2 * EXPERTS * D * vocab,
        moved=4 << 20,
        unused=[in_hbm(part) for part in sent],
    )
    to_own = call(
        sums_kernel,
        [],
        [heads, lm_head],
        like((vocab, EXPERTS), f32),
        flops=2 * EXPERTS * D * vocab,
        moved=4 << 20,
    )
    logits, stats = call(
        logits_kernel,
        [core_at],
        [to_own, swap(to_other)],
        [pltpu.HBM((2, vocab, EXPERTS), f32), pltpu.HBM((32, 4, EXPERTS), f32)],
        moved=1 << 20,
    )
    mixture = own
    for part in sent:
        mixture = mixture + part.astype(f32)
    layer_out = (hidden.astype(f32) + mixture).astype(bf16)
    stats = exchange(stats, ("x", "y", "c"))
    stats = call(merge_kernel, [], [stats], pltpu.HBM((NZ, 4, EXPERTS), f32))
    stats = exchange(stats, "z")
    logprob = call(finish_kernel, [], [stats, in_hbm(logits)], like((2, vocab, EXPERTS), f32))
    return (attended, layer_out, jnp.transpose(logprob, (0, 2, 1)))


def solution(mesh):
    fine = Mesh(mesh.devices.reshape(4, 8, 4, 2), ALL)
    in_specs = (
        P(EP, None, TP),
        P(None, EP, None, TP),
        P(None, EP, None, TP),
        P(EP),
        P(EP, None),
        P(EP, TP),
        P(),
        P(EP, None),
        P(EP, None),
        P(EP, None, TP),
        P(EP, None, TP),
        P(EP, TP, None),
        P(EP),
        P(),
        P(None, ALL, None),
        P(None, ALL),
        P(ALL, None),
    )
    out_specs = (P(EP, None, TP), P(EP, TP), P(None, None, ALL))
    return jax.shard_map(
        on_device, mesh=fine, in_specs=in_specs, out_specs=out_specs, check_vma=False
    )
```

```python
import jax
import jax.numpy as jnp
from jax import lax
from jax.experimental import pallas as pl
from jax.experimental.pallas import tpu as pltpu
from jax.sharding import Mesh, PartitionSpec as P

HD = 128
TOPK = 8
NODES = 32
CAP = 4
EXPERTS = 128
D = 4096
HALF = D // 2

eps_norm = 1e-06
EP = ("x", "z", "y")
TP = "c"
ALL = ("x", "z", "y", "c")
PLANE = ("x", "y")
NZ = 8
NY = 4
NPLANE = 16
LANES = 128
NEAR = (1, 2, -1, -2)
BLOCK = 512
VMEM_LIMIT = 24 << 20
SWAP = [(0, 1), (1, 0)]


def swap(value):
    return lax.ppermute(value, TP, SWAP)


def around(count, step):
    return [(chip, (chip + step) % count) for chip in range(count)]


def exchange(value, axes):
    return lax.all_to_all(value, axes, 0, 0, tiled=True)


def dot32(left, right):
    return jnp.dot(left, right, preferred_element_type=jnp.float32)


def last_dot(left, right):
    return lax.dot_general(
        left, right, (((1,), (1,)), ((), ())), preferred_element_type=jnp.float32
    )


def first_dot(left, right):
    return lax.dot_general(
        left, right, (((0,), (0,)), ((), ())), preferred_element_type=jnp.float32
    )


def iota(shape, dim):
    return lax.broadcasted_iota(jnp.int32, shape, dim)


def as_bf16(mask):
    return mask.astype(jnp.float32).astype(jnp.bfloat16)


def as_column(row):
    count = row.shape[1]
    here = iota((count, count), 0) == iota((count, count), 1)
    return jnp.sum(jnp.where(here, row, 0.0), 1, keepdims=True)


def silu(value):
    return value / (1.0 + jnp.exp(-value))


SMEM = pl.BlockSpec(memory_space=pltpu.SMEM)
ANY = pl.BlockSpec(memory_space=pl.ANY)


def whole(array):
    return pl.BlockSpec(array.shape, lambda *_: (0,) * len(array.shape))


def in_hbm(array):
    return pltpu.with_memory_space_constraint(array, pltpu.HBM)


def in_vmem(array):
    return pltpu.with_memory_space_constraint(array, pltpu.VMEM)


def like(shape, dtype):
    return jax.ShapeDtypeStruct(shape, dtype)


def call(kernel, scalars, arrays, out_shape, flops=0, moved=1 << 20, unused=(), scratch=()):
    outs = out_shape if isinstance(out_shape, (list, tuple)) else [out_shape]
    count = len(scalars)

    def body(*refs):
        rest = refs[count + len(arrays) + len(unused) :]
        kernel(*refs[: count + len(arrays)], *rest)

    result = pl.pallas_call(
        body,
        out_shape=list(outs),
        in_specs=[SMEM] * count + [whole(a) for a in arrays] + [ANY] * len(unused),
        out_specs=[whole(o) for o in outs],
        scratch_shapes=list(scratch),
        compiler_params=pltpu.CompilerParams(vmem_limit_bytes=VMEM_LIMIT),
        cost_estimate=pl.CostEstimate(flops=flops, bytes_accessed=moved, transcendentals=0),
    )(*scalars, *arrays, *unused)
    return result if isinstance(out_shape, (list, tuple)) else result[0]


def attention_kernel(length, query, new_kv, cache, parents, attended):
    nodes = query.shape[1]
    heads = query.shape[2] // HD
    kv_heads = cache.shape[3] // HD
    group = heads // kv_heads
    shape = (nodes, nodes)
    parent = as_column(parents[...].astype(jnp.float32))
    column = iota(shape, 1).astype(jnp.float32)
    reach = ((column == parent) | (iota(shape, 0) == iota(shape, 1))).astype(jnp.float32)
    for _ in range(5):
        reach = jnp.minimum(dot32(reach.astype(jnp.bfloat16), reach.astype(jnp.bfloat16)), 1.0)
    reach = jnp.concatenate([reach] * group, 0)
    for kv in range(kv_heads):
        here = pl.ds(kv * HD, HD)
        first = kv * group
        rows = [query[0, :, (first + h) * HD : (first + h + 1) * HD] for h in range(group)]
        rows = jnp.concatenate(rows, 0)
        old = last_dot(rows, cache[0, 0, :, here]) * HD ** (-0.5)
        new = last_dot(rows, new_kv[0, 0, :, here]) * HD ** (-0.5)
        old = jnp.where(iota(old.shape, 1) < length[0], old, -jnp.inf)
        new = jnp.where(reach > 0.5, new, -jnp.inf)
        top = jnp.maximum(jnp.max(old, -1, keepdims=True), jnp.max(new, -1, keepdims=True))
        old, new = jnp.exp(old - top), jnp.exp(new - top)
        total = jnp.sum(old, -1, keepdims=True) + jnp.sum(new, -1, keepdims=True)
        mixed = dot32((old / total).astype(jnp.bfloat16), cache[1, 0, :, here])
        mixed = mixed + dot32((new / total).astype(jnp.bfloat16), new_kv[1, 0, :, here])
        mixed = mixed.astype(jnp.bfloat16)
        for h in range(group):
            attended[0, :, (first + h) * HD : (first + h + 1) * HD] = mixed[
                h * nodes : (h + 1) * nodes
            ]


def begin_kernel(accept, hidden, routes, gates, packet):
    share = gates[...] / jnp.sum(gates[...], 0, keepdims=True)
    share_hi = share.astype(jnp.bfloat16).astype(jnp.float32)
    flag = (iota((TOPK, NODES), 1) == accept[0]).astype(jnp.float32)
    stack = [routes[...].astype(jnp.float32), share_hi, share - share_hi, flag]
    stack = jnp.concatenate(stack, 0).astype(jnp.bfloat16)
    here = iota((NODES, LANES), 0) == iota((NODES, LANES), 1)
    notes = first_dot(stack, as_bf16(here)).astype(jnp.bfloat16)
    for chip in range(NZ):
        packet[chip, :, :HALF] = hidden[...]
        packet[chip, :, HALF:] = notes


def widen_kernel(weights, bias, wide):
    block = weights.shape[1]
    lane = iota((block, LANES), 1)
    for head in range(2):
        wide[head, :, :D] = weights[head]
        value = as_column(bias[head : head + 1, :])
        extra = jnp.zeros((block, LANES), jnp.float32)
        for place in range(3):
            part = value.astype(jnp.bfloat16).astype(jnp.float32)
            extra = jnp.where(lane == place, part, extra)
            value = value - part
        wide[head, :, D:] = extra.astype(jnp.bfloat16)


def assemble_kernel(core, my_y, *refs):
    own, other, weights = refs[:NY], refs[NY], refs[NY + 1]
    block = own[0].shape[1]
    for step in range(NY):
        place = lax.rem(my_y[0] - step + NY, NY) * 2
        for head in range(2):
            here = pl.ds(pl.multiple_of((place + core[0]) * block, block), block)
            weights[head, here, :] = own[step][head]
            here = pl.ds(pl.multiple_of((place + 1 - core[0]) * block, block), block)
            weights[head, here, :] = other[step, head]


def route_kernel(my_z, column, outgoing, mix_hi, mix_lo, accepted_mix):
    count = NZ * NODES
    slots = NZ * CAP
    tokens = column[...].reshape(count, HALF + LANES)
    turn = as_bf16(iota((NODES, LANES), 0) == iota((NODES, LANES), 1))
    notes = last_dot(turn, tokens[:, HALF:])
    expert = iota((NPLANE, 1), 0)
    expert = (((expert // 4) * NZ + my_z[0]) * 4 + expert % 4).astype(jnp.float32)
    member = jnp.zeros((NPLANE, count), jnp.float32)
    share_hi, share_lo = member, member
    for pick in range(TOPK):
        match = (notes[pick : pick + 1] == expert).astype(jnp.float32)
        member = member + match
        share_hi = share_hi + match * notes[TOPK + pick : TOPK + pick + 1]
        share_lo = share_lo + match * notes[2 * TOPK + pick : 2 * TOPK + pick + 1]
    first, second = iota((count, count), 0), iota((count, count), 1)
    earlier = (first < second) & (first // NODES == second // NODES)
    rank = dot32(member.astype(jnp.bfloat16), as_bf16(earlier))
    source = iota((1, count), 1) // NODES
    slot = jnp.where(member > 0.5, (source * CAP).astype(jnp.float32) + rank, -1.0)
    wanted = iota((slots, 1), 0).astype(jnp.float32)
    chosen = []
    for place in range(NPLANE):
        one = (slot[place : place + 1] == wanted).astype(jnp.float32)
        here = pl.ds(place * slots, slots)
        mix_hi[here, :] = (one * share_hi[place : place + 1]).astype(jnp.bfloat16)
        mix_lo[here, :] = (one * share_lo[place : place + 1]).astype(jnp.bfloat16)
        chosen.append(one.astype(jnp.bfloat16))
    chosen = jnp.concatenate(chosen, 0)
    for piece in range(HALF // BLOCK):
        here = slice(piece * BLOCK, (piece + 1) * BLOCK)
        part = dot32(chosen, tokens[:, here]).astype(jnp.bfloat16)
        outgoing[:, :, here] = part.reshape(NPLANE, slots, BLOCK)
    flag = notes[3 * TOPK : 3 * TOPK + 1]
    accepted = jnp.where(source == iota((NZ, 1), 0), flag, 0.0).astype(jnp.bfloat16)
    accepted_mix[:NZ] = last_dot(accepted, mix_hi[...]).astype(jnp.bfloat16)
    accepted_mix[NZ:] = last_dot(accepted, mix_lo[...]).astype(jnp.bfloat16)


def squares_kernel(arrived, squares):
    count = squares.shape[0] * LANES
    total = jnp.zeros((count, LANES), jnp.float32)
    for tile in range(HALF // LANES):
        here = slice(tile * LANES, (tile + 1) * LANES)
        values = arrived[:, :, here].reshape(count, LANES).astype(jnp.float32)
        total = total + values * values
    total = jnp.sum(total, -1, keepdims=True)
    here = iota((LANES, LANES), 0) == iota((LANES, LANES), 1)
    for place in range(squares.shape[0]):
        part = total[place * LANES : (place + 1) * LANES]
        squares[place : place + 1, :] = jnp.sum(jnp.where(here, part, 0.0), 0, keepdims=True)


def half_sums(core, arrived, own, other, gain, w_gate, w_up, rows):
    count = rows.shape[0]
    tiles = HALF // LANES
    sums = own[...] + other[...]
    sums = [as_column(sums[place : place + 1, :]) for place in range(count // LANES)]
    factor = lax.rsqrt(jnp.concatenate(sums, 0) / D + eps_norm)
    for tile in range(tiles):
        here = slice(tile * LANES, (tile + 1) * LANES)
        values = arrived[:, :, here].reshape(count, LANES).astype(jnp.float32)
        values = values * factor * gain[pl.ds(core * tiles + tile, 1), :]
        rows[:, here] = values.astype(jnp.bfloat16)
    here = pl.ds(pl.multiple_of(core * HALF, HALF), HALF)
    return dot32(rows[...], w_gate[0, here, :]), dot32(rows[...], w_up[0, here, :])


def first_half_kernel(core, arrived, own, other, gain, w_gate, w_up, gate, up, rows):
    gate[...], up[...] = half_sums(core[0], arrived, own, other, gain, w_gate, w_up, rows)


def second_half_kernel(
    core, arrived, own, other, gain, w_gate, w_up, gate, up, activation, rows
):
    gate_part, up_part = half_sums(1 - core[0], arrived, own, other, gain, w_gate, w_up, rows)
    activation[...] = (silu(gate[...] + gate_part) * (up[...] + up_part)).astype(jnp.bfloat16)


def own_down_kernel(core, own, down, part):
    for piece in range(HALF // BLOCK):
        here = slice(piece * BLOCK, (piece + 1) * BLOCK)
        columns = pl.ds(pl.multiple_of(core[0] * HALF + piece * BLOCK, BLOCK), BLOCK)
        part[:, here] = dot32(own[...], down[0, :, columns])


def other_down_kernel(part, other, other_down, finished):
    for piece in range(HALF // BLOCK):
        here = slice(piece * BLOCK, (piece + 1) * BLOCK)
        whole_sum = part[:, here] + dot32(other[...], other_down[:, here])
        finished[:, :, here] = whole_sum.astype(jnp.bfloat16).reshape(NPLANE, NZ * CAP, BLOCK)


def combine_kernel(
    accept, my_z, mix, mix_hi, mix_lo, returned, hidden, parts, own, far_up, far_down, near, total
):
    rows = returned[...].reshape(-1, HALF)
    part = dot32(mix[...], rows)
    part = part[:NZ] + part[NZ:]
    here = iota((NODES, 1), 0) == accept[0]
    row = jnp.sum(jnp.where(here, hidden[...].astype(jnp.float32), 0.0), 0, keepdims=True)
    part = part + jnp.where(iota((NZ, 1), 0) == my_z[0], row, 0.0)
    quarter = HALF // 2
    for core in range(2):
        four = part[core * 4 : core * 4 + 4]
        four = jnp.concatenate([four[:, :quarter], four[:, quarter:]], 0).astype(jnp.bfloat16)
        for chip in range(NZ):
            parts[chip * 2 + core] = four
    total[...] = first_dot(mix_hi[...], rows) + first_dot(mix_lo[...], rows)

    def block(step, first=0, count=NODES):
        place = lax.rem(my_z[0] + step + NZ, NZ)
        return total[pl.ds(pl.multiple_of(place * NODES + first, 16), count), :]

    own[...] = block(0)
    far_up[:NODES, :] = block(3).astype(jnp.bfloat16)
    far_up[NODES:, :] = block(4, 0, NODES // 2).astype(jnp.bfloat16)
    far_down[:NODES, :] = block(-3).astype(jnp.bfloat16)
    far_down[NODES:, :] = block(4, NODES // 2, NODES // 2).astype(jnp.bfloat16)
    for place, step in enumerate(NEAR):
        near[place] = block(step)


def relay_kernel(near, from_below, from_above, up1, up2, down1, down2):
    half = NODES // 2
    below, above = from_below[...].astype(jnp.float32), from_above[...].astype(jnp.float32)
    up1[...] = (near[0] + below[:NODES]).astype(jnp.bfloat16)
    up2[:half, :] = (near[1, :half] + below[NODES:]).astype(jnp.bfloat16)
    up2[half:, :] = near[1, half:].astype(jnp.bfloat16)
    down1[...] = (near[2] + above[:NODES]).astype(jnp.bfloat16)
    down2[:half, :] = near[3, :half].astype(jnp.bfloat16)
    down2[half:, :] = (near[3, half:] + above[NODES:]).astype(jnp.bfloat16)


def final_kernel(parts, gain, copies):
    quarter = parts.shape[2]
    chosen = jnp.sum(parts[...].reshape(NZ, 2, 8, quarter).astype(jnp.float32), 0)
    chosen = chosen.astype(jnp.bfloat16).astype(jnp.float32)
    squares = jnp.sum(jnp.sum(chosen * chosen, -1, keepdims=True), 0)
    squares = squares + jnp.concatenate([squares[4:], squares[:4]], 0)
    factor = lax.rsqrt(squares / D + eps_norm)
    first = iota((8, 1), 0) < 4
    tiles = quarter // LANES
    for core in range(2):
        for tile in range(tiles):
            low = core * 2 * tiles + tile
            own_gain = jnp.where(first, gain[low : low + 1], gain[low + tiles : low + tiles + 1])
            here = slice(tile * LANES, (tile + 1) * LANES)
            final = (chosen[core, :, here] * factor * own_gain).astype(jnp.bfloat16)
            for chip in range(copies.shape[0]):
                copies[chip, core * 8 : (core + 1) * 8, here] = final


def medusa_kernel(tile, final, weights, copies):
    count, quarter = final.shape[0] * final.shape[1], final.shape[2]
    shape = (count // 4, count)
    row = iota(shape, 0)

    def pick(part):
        return as_bf16(iota(shape, 1) == row // 4 * 16 + part * 4 + row % 4)

    pieces = final[...].reshape(count, quarter)
    rows = [dot32(pick(part), pieces).astype(jnp.bfloat16) for part in range(4)]
    here = pl.ds(pl.multiple_of(tile[0] % NZ * LANES, LANES), LANES)
    own = dot32(pick(tile[0] // NZ), final[:, :, here].reshape(count, LANES))
    rows.append(as_bf16(iota((count // 4, LANES), 1) < 3))
    rows = jnp.concatenate(rows, 1)
    heads = [own + silu(last_dot(rows, weights[head])) for head in range(2)]
    heads = jnp.concatenate(heads, 0).astype(jnp.bfloat16)
    for chip in range(NZ):
        copies[chip] = heads


def copy_kernel(heads, copies):
    for chip in range(NPLANE):
        copies[chip] = heads[...]


def head_sums(heads, lm):
    tiles = []
    for x in range(4):
        for z in range(NZ):
            tiles.append(jnp.concatenate([heads[x * NY + y, z] for y in range(NY)], 0))
    return last_dot(lm[...], jnp.concatenate(tiles, 1))


def sums_kernel(heads, lm, total):
    total[...] = head_sums(heads, lm)


def logits_kernel(core, own, other, logits, stats):
    both = jnp.concatenate([own[...], other[...]], 1)
    shape = (2 * EXPERTS, 2 * EXPERTS)
    lane = iota(shape, 0)
    z = jnp.where(lane < EXPERTS, core[0], 1 - core[0]) * 4 + lane % 4
    wanted = lane // 16 % 2 * EXPERTS + lane // 4 % 4 * 32 + z * 4 + lane // 32 % 4
    order = as_bf16(wanted == iota(shape, 1))
    total = jnp.zeros(both.shape, jnp.float32)
    for _ in range(3):
        part = both.astype(jnp.bfloat16)
        total = total + dot32(part, order)
        both = both - part.astype(jnp.float32)
    top = jnp.max(total, 0, keepdims=True)
    sums = jnp.sum(jnp.exp(total - top), 0, keepdims=True)
    for head in range(2):
        here = slice(head * EXPERTS, (head + 1) * EXPERTS)
        logits[head] = total[:, here]
        for place in range(stats.shape[0]):
            stats[place, head : head + 1, :] = top[:, here]
            stats[place, 2 + head : 3 + head, :] = sums[:, here]


def merged(stats):
    tops, sums = stats[:, :2], stats[:, 2:]
    top = jnp.max(tops, 0)
    return top, jnp.sum(sums * jnp.exp(tops - top[None]), 0)


def merge_kernel(stats, copies):
    top, sums = merged(stats[...])
    for chip in range(NZ):
        copies[chip, :2, :] = top
        copies[chip, 2:, :] = sums


def finish_kernel(stats, logits, logprob):
    top, sums = merged(stats[...])
    shift = top + jnp.log(sums)
    for head in range(2):
        logprob[head] = logits[head] - shift[head : head + 1, :]


def on_device(
    query,
    new_kv,
    cache,
    cache_len,
    parents,
    hidden,
    moe_gain,
    routes,
    gates,
    w_gate,
    w_up,
    w_down,
    accept,
    final_gain,
    medusa_w,
    medusa_b,
    lm_head,
):
    bf16, f32 = jnp.bfloat16, jnp.float32
    core, my_z = lax.axis_index(TP), lax.axis_index("z")
    core_at, z_at, y_at = core.reshape(1), my_z.reshape(1), lax.axis_index("y").reshape(1)
    tile_at = (lax.axis_index("x") * NZ + my_z).reshape(1)
    slots = NPLANE * NZ * CAP
    units = w_gate.shape[2]
    vocab = lm_head.shape[0]

    packet = call(
        begin_kernel,
        [accept],
        [in_hbm(hidden), in_hbm(routes.T), in_hbm(gates.T)],
        pltpu.HBM((NZ, NODES, HALF + LANES), bf16),
    )
    column = exchange(packet, "z")

    attended = call(
        attention_kernel,
        [cache_len],
        [query, new_kv, cache, parents],
        like(query.shape, bf16),
        flops=4 << 24,
        moved=4 << 20,
    )
    wide_w = call(
        widen_kernel,
        [],
        [in_hbm(medusa_w), in_hbm(medusa_b)],
        like(medusa_w.shape[:2] + (D + LANES,), bf16),
    )
    wide = [wide_w] + [lax.ppermute(wide_w, "y", around(NY, step)) for step in range(1, NY)]
    block_w = call(
        assemble_kernel,
        [core_at, y_at],
        wide + [swap(jnp.stack(wide))],
        pltpu.HBM((2, LANES, D + LANES), bf16),
        moved=4 << 20,
    )
    other_down = swap(lax.dynamic_slice_in_dim(w_down[0], (1 - core) * HALF, HALF, 1))

    other_lm = swap(lm_head)

    outgoing, mix_hi, mix_lo, accepted_mix = call(
        route_kernel,
        [z_at],
        [column],
        [
            pltpu.VMEM((NPLANE, NZ * CAP, HALF), bf16),
            pltpu.HBM((slots, NZ * NODES), bf16),
            pltpu.HBM((slots, NZ * NODES), bf16),
            like((2 * NZ, slots), bf16),
        ],
        flops=2 * slots * NZ * NODES * HALF,
        moved=4 << 20,
        unused=[in_hbm(attended), in_hbm(block_w), in_hbm(other_down), other_lm],
    )
    arrived = exchange(outgoing, PLANE)
    squares = call(squares_kernel, [], [arrived], like((slots // LANES, LANES), f32))
    both = [squares, swap(squares)]
    gain = moe_gain.reshape(-1, LANES)
    sums = call(
        first_half_kernel,
        [core_at],
        [arrived, *both, gain, w_gate, w_up],
        [like((slots, units), f32)] * 2,
        flops=4 * slots * HALF * units,
        moved=8 << 20,
        scratch=[pltpu.VMEM((slots, HALF), bf16)],
    )
    activation = call(
        second_half_kernel,
        [core_at],
        [swap(arrived), *both, gain, w_gate, w_up, *sums],
        like((slots, units), bf16),
        flops=4 * slots * HALF * units,
        moved=8 << 20,
        scratch=[pltpu.VMEM((slots, HALF), bf16)],
    )
    part = call(
        own_down_kernel,
        [core_at],
        [activation, w_down],
        like((slots, HALF), f32),
        flops=2 * slots * HALF * units,
        moved=6 << 20,
    )
    finished = call(
        other_down_kernel,
        [],
        [part, swap(activation), other_down],
        pltpu.VMEM((NPLANE, NZ * CAP, HALF), bf16),
        flops=2 * slots * HALF * units,
        moved=6 << 20,
    )
    returned = exchange(finished, PLANE)

    parts, own, far_up, far_down, near = call(
        combine_kernel,
        [accept, z_at],
        [accepted_mix, in_hbm(mix_hi), in_hbm(mix_lo), returned, hidden],
        [
            pltpu.HBM((2 * NZ, NZ, HALF // 2), bf16),
            pltpu.HBM((NODES, HALF), f32),
            pltpu.HBM((NODES * 3 // 2, HALF), bf16),
            pltpu.HBM((NODES * 3 // 2, HALF), bf16),
            pltpu.HBM((len(NEAR), NODES, HALF), f32),
        ],
        flops=4 * slots * NZ * NODES * HALF,
        moved=6 << 20,
        scratch=[pltpu.VMEM((NZ * NODES, HALF), f32)],
    )
    parts = exchange(parts, ("z", "c"))
    from_below = in_hbm(lax.ppermute(far_up, "z", around(NZ, 2)))
    from_above = in_hbm(lax.ppermute(far_down, "z", around(NZ, -2)))
    relayed = call(
        relay_kernel,
        [],
        [in_hbm(near), from_below, from_above],
        [pltpu.HBM((NODES, HALF), bf16)] * len(NEAR),
        moved=2 << 20,
    )
    sent = [
        lax.ppermute(part, "z", around(NZ, step)) for step, part in zip(NEAR, relayed)
    ]

    final = call(
        final_kernel,
        [],
        [parts, in_hbm(final_gain.reshape(-1, LANES))],
        pltpu.HBM((4, 16, HALF // 2), bf16),
    )
    final = exchange(final, "x")
    heads = call(
        medusa_kernel,
        [tile_at],
        [final, block_w],
        pltpu.HBM((NZ, 32, LANES), bf16),
        flops=2 * 16 * D * 256,
        moved=3 << 20,
    )
    heads = exchange(heads, "z")
    heads = call(
        copy_kernel,
        [],
        [heads],
        pltpu.HBM((NPLANE, NZ, 32, LANES), bf16),
        unused=[in_hbm(relayed[0])],
    )
    heads = exchange(heads, PLANE)
    to_other = call(
        sums_kernel,
        [],
        [heads, other_lm],
        like((vocab, EXPERTS), f32),
        flops=2 * EXPERTS * D * vocab,
        moved=4 << 20,
        unused=[in_hbm(part) for part in sent],
    )
    to_own = call(
        sums_kernel,
        [],
        [heads, lm_head],
        like((vocab, EXPERTS), f32),
        flops=2 * EXPERTS * D * vocab,
        moved=4 << 20,
    )
    logits, stats = call(
        logits_kernel,
        [core_at],
        [to_own, swap(to_other)],
        [pltpu.HBM((2, vocab, EXPERTS), f32), pltpu.HBM((32, 4, EXPERTS), f32)],
        moved=1 << 20,
    )
    mixture = own
    for part in sent:
        mixture = mixture + part.astype(f32)
    layer_out = (hidden.astype(f32) + mixture).astype(bf16)
    stats = exchange(stats, ("x", "y", "c"))
    stats = call(merge_kernel, [], [stats], pltpu.HBM((NZ, 4, EXPERTS), f32))
    stats = exchange(stats, "z")
    logprob = call(finish_kernel, [], [stats, in_hbm(logits)], like((2, vocab, EXPERTS), f32))
    return (attended, layer_out, jnp.transpose(logprob, (0, 2, 1)))


def solution(mesh):
    fine = Mesh(mesh.devices.reshape(4, 8, 4, 2), ALL)
    in_specs = (
        P(EP, None, TP),
        P(None, EP, None, TP),
        P(None, EP, None, TP),
        P(EP),
        P(EP, None),
        P(EP, TP),
        P(),
        P(EP, None),
        P(EP, None),
        P(EP, None, TP),
        P(EP, None, TP),
        P(EP, TP, None),
        P(EP),
        P(),
        P(None, ALL, None),
        P(None, ALL),
        P(ALL, None),
    )
    out_specs = (P(EP, None, TP), P(EP, TP), P(None, None, ALL))
    return jax.shard_map(
        on_device, mesh=fine, in_specs=in_specs, out_specs=out_specs, check_vma=False
    )
```

```python
import jax
import jax.numpy as jnp
from jax import lax
from jax.experimental import pallas as pl
from jax.experimental.pallas import tpu as pltpu
from jax.sharding import Mesh, PartitionSpec as P

HD = 128
TOPK = 8
NODES = 32
CAP = 4
EXPERTS = 128
D = 4096
HALF = D // 2

eps_norm = 1e-06
EP = ("x", "z", "y")
TP = "c"
ALL = ("x", "z", "y", "c")
PLANE = ("x", "y")
NZ = 8
NY = 4
NPLANE = 16
LANES = 128
NEAR = (1, 2, -1, -2)
BLOCK = 512
VMEM_LIMIT = 24 << 20
SWAP = [(0, 1), (1, 0)]


def swap(value):
    return lax.ppermute(value, TP, SWAP)


def around(count, step):
    return [(chip, (chip + step) % count) for chip in range(count)]


def exchange(value, axes):
    return lax.all_to_all(value, axes, 0, 0, tiled=True)


def dot32(left, right):
    return jnp.dot(left, right, preferred_element_type=jnp.float32)


def last_dot(left, right):
    return lax.dot_general(
        left, right, (((1,), (1,)), ((), ())), preferred_element_type=jnp.float32
    )


def first_dot(left, right):
    return lax.dot_general(
        left, right, (((0,), (0,)), ((), ())), preferred_element_type=jnp.float32
    )


def iota(shape, dim):
    return lax.broadcasted_iota(jnp.int32, shape, dim)


def as_bf16(mask):
    return mask.astype(jnp.float32).astype(jnp.bfloat16)


def as_column(row):
    count = row.shape[1]
    here = iota((count, count), 0) == iota((count, count), 1)
    return jnp.sum(jnp.where(here, row, 0.0), 1, keepdims=True)


def silu(value):
    return value / (1.0 + jnp.exp(-value))


SMEM = pl.BlockSpec(memory_space=pltpu.SMEM)
ANY = pl.BlockSpec(memory_space=pl.ANY)


def whole(array):
    return pl.BlockSpec(array.shape, lambda *_: (0,) * len(array.shape))


def in_hbm(array):
    return pltpu.with_memory_space_constraint(array, pltpu.HBM)


def in_vmem(array):
    return pltpu.with_memory_space_constraint(array, pltpu.VMEM)


def like(shape, dtype):
    return jax.ShapeDtypeStruct(shape, dtype)


def call(kernel, scalars, arrays, out_shape, flops=0, moved=1 << 20, unused=(), scratch=()):
    outs = out_shape if isinstance(out_shape, (list, tuple)) else [out_shape]
    count = len(scalars)

    def body(*refs):
        rest = refs[count + len(arrays) + len(unused) :]
        kernel(*refs[: count + len(arrays)], *rest)

    result = pl.pallas_call(
        body,
        out_shape=list(outs),
        in_specs=[SMEM] * count + [whole(a) for a in arrays] + [ANY] * len(unused),
        out_specs=[whole(o) for o in outs],
        scratch_shapes=list(scratch),
        compiler_params=pltpu.CompilerParams(vmem_limit_bytes=VMEM_LIMIT),
        cost_estimate=pl.CostEstimate(flops=flops, bytes_accessed=moved, transcendentals=0),
    )(*scalars, *arrays, *unused)
    return result if isinstance(out_shape, (list, tuple)) else result[0]


def attention_kernel(length, query, new_kv, cache, parents, attended):
    nodes = query.shape[1]
    heads = query.shape[2] // HD
    kv_heads = cache.shape[3] // HD
    group = heads // kv_heads
    shape = (nodes, nodes)
    parent = as_column(parents[...].astype(jnp.float32))
    column = iota(shape, 1).astype(jnp.float32)
    reach = ((column == parent) | (iota(shape, 0) == iota(shape, 1))).astype(jnp.float32)
    for _ in range(5):
        reach = jnp.minimum(dot32(reach.astype(jnp.bfloat16), reach.astype(jnp.bfloat16)), 1.0)
    reach = jnp.concatenate([reach] * group, 0)
    for kv in range(kv_heads):
        here = pl.ds(kv * HD, HD)
        first = kv * group
        rows = [query[0, :, (first + h) * HD : (first + h + 1) * HD] for h in range(group)]
        rows = jnp.concatenate(rows, 0)
        old = last_dot(rows, cache[0, 0, :, here]) * HD ** (-0.5)
        new = last_dot(rows, new_kv[0, 0, :, here]) * HD ** (-0.5)
        old = jnp.where(iota(old.shape, 1) < length[0], old, -jnp.inf)
        new = jnp.where(reach > 0.5, new, -jnp.inf)
        top = jnp.maximum(jnp.max(old, -1, keepdims=True), jnp.max(new, -1, keepdims=True))
        old, new = jnp.exp(old - top), jnp.exp(new - top)
        total = jnp.sum(old, -1, keepdims=True) + jnp.sum(new, -1, keepdims=True)
        mixed = dot32((old / total).astype(jnp.bfloat16), cache[1, 0, :, here])
        mixed = mixed + dot32((new / total).astype(jnp.bfloat16), new_kv[1, 0, :, here])
        mixed = mixed.astype(jnp.bfloat16)
        for h in range(group):
            attended[0, :, (first + h) * HD : (first + h + 1) * HD] = mixed[
                h * nodes : (h + 1) * nodes
            ]


def begin_kernel(accept, hidden, routes, gates, packet):
    share = gates[...] / jnp.sum(gates[...], 0, keepdims=True)
    share_hi = share.astype(jnp.bfloat16).astype(jnp.float32)
    flag = (iota((TOPK, NODES), 1) == accept[0]).astype(jnp.float32)
    stack = [routes[...].astype(jnp.float32), share_hi, share - share_hi, flag]
    stack = jnp.concatenate(stack, 0).astype(jnp.bfloat16)
    here = iota((NODES, LANES), 0) == iota((NODES, LANES), 1)
    notes = first_dot(stack, as_bf16(here)).astype(jnp.bfloat16)
    for chip in range(NZ):
        packet[chip, :, :HALF] = hidden[...]
        packet[chip, :, HALF:] = notes


def widen_kernel(weights, bias, wide):
    block = weights.shape[1]
    lane = iota((block, LANES), 1)
    for head in range(2):
        wide[head, :, :D] = weights[head]
        value = as_column(bias[head : head + 1, :])
        extra = jnp.zeros((block, LANES), jnp.float32)
        for place in range(3):
            part = value.astype(jnp.bfloat16).astype(jnp.float32)
            extra = jnp.where(lane == place, part, extra)
            value = value - part
        wide[head, :, D:] = extra.astype(jnp.bfloat16)


def assemble_kernel(core, my_y, *refs):
    own, other, weights = refs[:NY], refs[NY], refs[NY + 1]
    block = own[0].shape[1]
    for step in range(NY):
        place = lax.rem(my_y[0] - step + NY, NY) * 2
        for head in range(2):
            here = pl.ds(pl.multiple_of((place + core[0]) * block, block), block)
            weights[head, here, :] = own[step][head]
            here = pl.ds(pl.multiple_of((place + 1 - core[0]) * block, block), block)
            weights[head, here, :] = other[step, head]


def route_kernel(my_z, column, outgoing, mix_hi, mix_lo, accepted_mix):
    count = NZ * NODES
    slots = NZ * CAP
    tokens = column[...].reshape(count, HALF + LANES)
    turn = as_bf16(iota((NODES, LANES), 0) == iota((NODES, LANES), 1))
    notes = last_dot(turn, tokens[:, HALF:])
    expert = iota((NPLANE, 1), 0)
    expert = (((expert // 4) * NZ + my_z[0]) * 4 + expert % 4).astype(jnp.float32)
    member = jnp.zeros((NPLANE, count), jnp.float32)
    share_hi, share_lo = member, member
    for pick in range(TOPK):
        match = (notes[pick : pick + 1] == expert).astype(jnp.float32)
        member = member + match
        share_hi = share_hi + match * notes[TOPK + pick : TOPK + pick + 1]
        share_lo = share_lo + match * notes[2 * TOPK + pick : 2 * TOPK + pick + 1]
    first, second = iota((count, count), 0), iota((count, count), 1)
    earlier = (first < second) & (first // NODES == second // NODES)
    rank = dot32(member.astype(jnp.bfloat16), as_bf16(earlier))
    source = iota((1, count), 1) // NODES
    slot = jnp.where(member > 0.5, (source * CAP).astype(jnp.float32) + rank, -1.0)
    wanted = iota((slots, 1), 0).astype(jnp.float32)
    chosen = []
    for place in range(NPLANE):
        one = (slot[place : place + 1] == wanted).astype(jnp.float32)
        here = pl.ds(place * slots, slots)
        mix_hi[here, :] = (one * share_hi[place : place + 1]).astype(jnp.bfloat16)
        mix_lo[here, :] = (one * share_lo[place : place + 1]).astype(jnp.bfloat16)
        chosen.append(one.astype(jnp.bfloat16))
    chosen = jnp.concatenate(chosen, 0)
    for piece in range(HALF // BLOCK):
        here = slice(piece * BLOCK, (piece + 1) * BLOCK)
        part = dot32(chosen, tokens[:, here]).astype(jnp.bfloat16)
        outgoing[:, :, here] = part.reshape(NPLANE, slots, BLOCK)
    flag = notes[3 * TOPK : 3 * TOPK + 1]
    accepted = jnp.where(source == iota((NZ, 1), 0), flag, 0.0).astype(jnp.bfloat16)
    accepted_mix[:NZ] = last_dot(accepted, mix_hi[...]).astype(jnp.bfloat16)
    accepted_mix[NZ:] = last_dot(accepted, mix_lo[...]).astype(jnp.bfloat16)


def squares_kernel(arrived, squares):
    count = squares.shape[0] * LANES
    total = jnp.zeros((count, LANES), jnp.float32)
    for tile in range(HALF // LANES):
        here = slice(tile * LANES, (tile + 1) * LANES)
        values = arrived[:, :, here].reshape(count, LANES).astype(jnp.float32)
        total = total + values * values
    total = jnp.sum(total, -1, keepdims=True)
    here = iota((LANES, LANES), 0) == iota((LANES, LANES), 1)
    for place in range(squares.shape[0]):
        part = total[place * LANES : (place + 1) * LANES]
        squares[place : place + 1, :] = jnp.sum(jnp.where(here, part, 0.0), 0, keepdims=True)


def half_sums(core, arrived, own, other, gain, w_gate, w_up, rows):
    count = rows.shape[0]
    tiles = HALF // LANES
    sums = own[...] + other[...]
    sums = [as_column(sums[place : place + 1, :]) for place in range(count // LANES)]
    factor = lax.rsqrt(jnp.concatenate(sums, 0) / D + eps_norm)
    for tile in range(tiles):
        here = slice(tile * LANES, (tile + 1) * LANES)
        values = arrived[:, :, here].reshape(count, LANES).astype(jnp.float32)
        values = values * factor * gain[pl.ds(core * tiles + tile, 1), :]
        rows[:, here] = values.astype(jnp.bfloat16)
    here = pl.ds(pl.multiple_of(core * HALF, HALF), HALF)
    return dot32(rows[...], w_gate[0, here, :]), dot32(rows[...], w_up[0, here, :])


def first_half_kernel(core, arrived, own, other, gain, w_gate, w_up, gate, up, rows):
    gate[...], up[...] = half_sums(core[0], arrived, own, other, gain, w_gate, w_up, rows)


def second_half_kernel(
    core, arrived, own, other, gain, w_gate, w_up, gate, up, activation, rows
):
    gate_part, up_part = half_sums(1 - core[0], arrived, own, other, gain, w_gate, w_up, rows)
    activation[...] = (silu(gate[...] + gate_part) * (up[...] + up_part)).astype(jnp.bfloat16)


def own_down_kernel(core, own, down, part):
    for piece in range(HALF // BLOCK):
        here = slice(piece * BLOCK, (piece + 1) * BLOCK)
        columns = pl.ds(pl.multiple_of(core[0] * HALF + piece * BLOCK, BLOCK), BLOCK)
        part[:, here] = dot32(own[...], down[0, :, columns])


def other_down_kernel(part, other, other_down, finished):
    for piece in range(HALF // BLOCK):
        here = slice(piece * BLOCK, (piece + 1) * BLOCK)
        whole_sum = part[:, here] + dot32(other[...], other_down[:, here])
        finished[:, :, here] = whole_sum.astype(jnp.bfloat16).reshape(NPLANE, NZ * CAP, BLOCK)


def combine_kernel(
    accept, my_z, mix, mix_hi, mix_lo, returned, hidden, parts, own, far_up, far_down, near, total
):
    rows = returned[...].reshape(-1, HALF)
    part = dot32(mix[...], rows)
    part = part[:NZ] + part[NZ:]
    here = iota((NODES, 1), 0) == accept[0]
    row = jnp.sum(jnp.where(here, hidden[...].astype(jnp.float32), 0.0), 0, keepdims=True)
    part = part + jnp.where(iota((NZ, 1), 0) == my_z[0], row, 0.0)
    quarter = HALF // 2
    for core in range(2):
        four = part[core * 4 : core * 4 + 4]
        four = jnp.concatenate([four[:, :quarter], four[:, quarter:]], 0).astype(jnp.bfloat16)
        for chip in range(NZ):
            parts[chip * 2 + core] = four
    total[...] = first_dot(mix_hi[...], rows) + first_dot(mix_lo[...], rows)

    def block(step, first=0, count=NODES):
        place = lax.rem(my_z[0] + step + NZ, NZ)
        return total[pl.ds(pl.multiple_of(place * NODES + first, 16), count), :]

    own[...] = block(0)
    far_up[:NODES, :] = block(3).astype(jnp.bfloat16)
    far_up[NODES:, :] = block(4, 0, NODES // 2).astype(jnp.bfloat16)
    far_down[:NODES, :] = block(-3).astype(jnp.bfloat16)
    far_down[NODES:, :] = block(4, NODES // 2, NODES // 2).astype(jnp.bfloat16)
    for place, step in enumerate(NEAR):
        near[place] = block(step)


def relay_kernel(near, from_below, from_above, up1, up2, down1, down2):
    half = NODES // 2
    below, above = from_below[...].astype(jnp.float32), from_above[...].astype(jnp.float32)
    up1[...] = (near[0] + below[:NODES]).astype(jnp.bfloat16)
    up2[:half, :] = (near[1, :half] + below[NODES:]).astype(jnp.bfloat16)
    up2[half:, :] = near[1, half:].astype(jnp.bfloat16)
    down1[...] = (near[2] + above[:NODES]).astype(jnp.bfloat16)
    down2[:half, :] = near[3, :half].astype(jnp.bfloat16)
    down2[half:, :] = (near[3, half:] + above[NODES:]).astype(jnp.bfloat16)


def final_kernel(parts, gain, copies):
    quarter = parts.shape[2]
    chosen = jnp.sum(parts[...].reshape(NZ, 2, 8, quarter).astype(jnp.float32), 0)
    chosen = chosen.astype(jnp.bfloat16).astype(jnp.float32)
    squares = jnp.sum(jnp.sum(chosen * chosen, -1, keepdims=True), 0)
    squares = squares + jnp.concatenate([squares[4:], squares[:4]], 0)
    factor = lax.rsqrt(squares / D + eps_norm)
    first = iota((8, 1), 0) < 4
    tiles = quarter // LANES
    for core in range(2):
        for tile in range(tiles):
            low = core * 2 * tiles + tile
            own_gain = jnp.where(first, gain[low : low + 1], gain[low + tiles : low + tiles + 1])
            here = slice(tile * LANES, (tile + 1) * LANES)
            final = (chosen[core, :, here] * factor * own_gain).astype(jnp.bfloat16)
            for chip in range(copies.shape[0]):
                copies[chip, core * 8 : (core + 1) * 8, here] = final


def medusa_kernel(tile, final, weights, copies):
    count, quarter = final.shape[0] * final.shape[1], final.shape[2]
    shape = (count // 4, count)
    row = iota(shape, 0)

    def pick(part):
        return as_bf16(iota(shape, 1) == row // 4 * 16 + part * 4 + row % 4)

    pieces = final[...].reshape(count, quarter)
    rows = [dot32(pick(part), pieces).astype(jnp.bfloat16) for part in range(4)]
    here = pl.ds(pl.multiple_of(tile[0] % NZ * LANES, LANES), LANES)
    own = dot32(pick(tile[0] // NZ), final[:, :, here].reshape(count, LANES))
    rows.append(as_bf16(iota((count // 4, LANES), 1) < 3))
    rows = jnp.concatenate(rows, 1)
    heads = [own + silu(last_dot(rows, weights[head])) for head in range(2)]
    heads = jnp.concatenate(heads, 0).astype(jnp.bfloat16)
    for chip in range(NZ):
        copies[chip] = heads


def copy_kernel(heads, copies):
    for chip in range(NPLANE):
        copies[chip] = heads[...]


def head_sums(heads, lm):
    tiles = []
    for x in range(4):
        for z in range(NZ):
            tiles.append(jnp.concatenate([heads[x * NY + y, z] for y in range(NY)], 0))
    return last_dot(lm[...], jnp.concatenate(tiles, 1))


def sums_kernel(heads, lm, total):
    total[...] = head_sums(heads, lm)


def logits_kernel(core, own, other, logits, stats):
    both = jnp.concatenate([own[...], other[...]], 1)
    shape = (2 * EXPERTS, 2 * EXPERTS)
    lane = iota(shape, 0)
    z = jnp.where(lane < EXPERTS, core[0], 1 - core[0]) * 4 + lane % 4
    wanted = lane // 16 % 2 * EXPERTS + lane // 4 % 4 * 32 + z * 4 + lane // 32 % 4
    order = as_bf16(wanted == iota(shape, 1))
    total = jnp.zeros(both.shape, jnp.float32)
    for _ in range(3):
        part = both.astype(jnp.bfloat16)
        total = total + dot32(part, order)
        both = both - part.astype(jnp.float32)
    top = jnp.max(total, 0, keepdims=True)
    sums = jnp.sum(jnp.exp(total - top), 0, keepdims=True)
    for head in range(2):
        here = slice(head * EXPERTS, (head + 1) * EXPERTS)
        logits[head] = total[:, here]
        for place in range(stats.shape[0]):
            stats[place, head : head + 1, :] = top[:, here]
            stats[place, 2 + head : 3 + head, :] = sums[:, here]


def merged(stats):
    tops, sums = stats[:, :2], stats[:, 2:]
    top = jnp.max(tops, 0)
    return top, jnp.sum(sums * jnp.exp(tops - top[None]), 0)


def merge_kernel(stats, copies):
    top, sums = merged(stats[...])
    for chip in range(NZ):
        copies[chip, :2, :] = top
        copies[chip, 2:, :] = sums


def finish_kernel(stats, logits, logprob):
    top, sums = merged(stats[...])
    shift = top + jnp.log(sums)
    own = jnp.where(pl.program_id(0) == 0, shift[0:1], shift[1:2])
    logprob[0] = logits[0] - own


def finish(stats, logits):
    head = pl.BlockSpec((1,) + logits.shape[1:], lambda i: (i, 0, 0))
    return pl.pallas_call(
        finish_kernel,
        out_shape=like(logits.shape, jnp.float32),
        grid=(2,),
        in_specs=[whole(stats), head],
        out_specs=head,
    )(stats, in_hbm(logits))


def on_device(
    query,
    new_kv,
    cache,
    cache_len,
    parents,
    hidden,
    moe_gain,
    routes,
    gates,
    w_gate,
    w_up,
    w_down,
    accept,
    final_gain,
    medusa_w,
    medusa_b,
    lm_head,
):
    bf16, f32 = jnp.bfloat16, jnp.float32
    core, my_z = lax.axis_index(TP), lax.axis_index("z")
    core_at, z_at, y_at = core.reshape(1), my_z.reshape(1), lax.axis_index("y").reshape(1)
    tile_at = (lax.axis_index("x") * NZ + my_z).reshape(1)
    slots = NPLANE * NZ * CAP
    units = w_gate.shape[2]
    vocab = lm_head.shape[0]

    packet = call(
        begin_kernel,
        [accept],
        [in_hbm(hidden), in_hbm(routes.T), in_hbm(gates.T)],
        pltpu.HBM((NZ, NODES, HALF + LANES), bf16),
    )
    column = exchange(packet, "z")

    attended = call(
        attention_kernel,
        [cache_len],
        [query, new_kv, cache, parents],
        like(query.shape, bf16),
        flops=4 << 24,
        moved=4 << 20,
    )
    wide_w = call(
        widen_kernel,
        [],
        [in_hbm(medusa_w), in_hbm(medusa_b)],
        like(medusa_w.shape[:2] + (D + LANES,), bf16),
    )
    wide = [wide_w] + [lax.ppermute(wide_w, "y", around(NY, step)) for step in range(1, NY)]
    block_w = call(
        assemble_kernel,
        [core_at, y_at],
        wide + [swap(jnp.stack(wide))],
        pltpu.HBM((2, LANES, D + LANES), bf16),
        moved=4 << 20,
    )
    other_down = swap(lax.dynamic_slice_in_dim(w_down[0], (1 - core) * HALF, HALF, 1))

    other_lm = swap(lm_head)

    outgoing, mix_hi, mix_lo, accepted_mix = call(
        route_kernel,
        [z_at],
        [column],
        [
            pltpu.VMEM((NPLANE, NZ * CAP, HALF), bf16),
            pltpu.HBM((slots, NZ * NODES), bf16),
            pltpu.HBM((slots, NZ * NODES), bf16),
            like((2 * NZ, slots), bf16),
        ],
        flops=2 * slots * NZ * NODES * HALF,
        moved=4 << 20,
        unused=[in_hbm(attended), in_hbm(block_w), in_hbm(other_down), other_lm],
    )
    arrived = exchange(outgoing, PLANE)
    squares = call(squares_kernel, [], [arrived], like((slots // LANES, LANES), f32))
    both = [squares, swap(squares)]
    gain = moe_gain.reshape(-1, LANES)
    sums = call(
        first_half_kernel,
        [core_at],
        [arrived, *both, gain, w_gate, w_up],
        [like((slots, units), f32)] * 2,
        flops=4 * slots * HALF * units,
        moved=8 << 20,
        scratch=[pltpu.VMEM((slots, HALF), bf16)],
    )
    activation = call(
        second_half_kernel,
        [core_at],
        [swap(arrived), *both, gain, w_gate, w_up, *sums],
        like((slots, units), bf16),
        flops=4 * slots * HALF * units,
        moved=8 << 20,
        scratch=[pltpu.VMEM((slots, HALF), bf16)],
    )
    part = call(
        own_down_kernel,
        [core_at],
        [activation, w_down],
        like((slots, HALF), f32),
        flops=2 * slots * HALF * units,
        moved=6 << 20,
    )
    finished = call(
        other_down_kernel,
        [],
        [part, swap(activation), other_down],
        pltpu.VMEM((NPLANE, NZ * CAP, HALF), bf16),
        flops=2 * slots * HALF * units,
        moved=6 << 20,
    )
    returned = exchange(finished, PLANE)

    parts, own, far_up, far_down, near = call(
        combine_kernel,
        [accept, z_at],
        [accepted_mix, in_hbm(mix_hi), in_hbm(mix_lo), returned, hidden],
        [
            pltpu.HBM((2 * NZ, NZ, HALF // 2), bf16),
            pltpu.HBM((NODES, HALF), f32),
            pltpu.HBM((NODES * 3 // 2, HALF), bf16),
            pltpu.HBM((NODES * 3 // 2, HALF), bf16),
            pltpu.HBM((len(NEAR), NODES, HALF), f32),
        ],
        flops=4 * slots * NZ * NODES * HALF,
        moved=6 << 20,
        scratch=[pltpu.VMEM((NZ * NODES, HALF), f32)],
    )
    parts = exchange(parts, ("z", "c"))
    from_below = in_hbm(lax.ppermute(far_up, "z", around(NZ, 2)))
    from_above = in_hbm(lax.ppermute(far_down, "z", around(NZ, -2)))
    relayed = call(
        relay_kernel,
        [],
        [in_hbm(near), from_below, from_above],
        [pltpu.HBM((NODES, HALF), bf16)] * len(NEAR),
        moved=2 << 20,
    )
    sent = [
        lax.ppermute(part, "z", around(NZ, step)) for step, part in zip(NEAR, relayed)
    ]

    final = call(
        final_kernel,
        [],
        [parts, in_hbm(final_gain.reshape(-1, LANES))],
        pltpu.HBM((4, 16, HALF // 2), bf16),
    )
    final = exchange(final, "x")
    heads = call(
        medusa_kernel,
        [tile_at],
        [final, block_w],
        pltpu.HBM((NZ, 32, LANES), bf16),
        flops=2 * 16 * D * 256,
        moved=3 << 20,
    )
    heads = exchange(heads, "z")
    heads = call(
        copy_kernel,
        [],
        [heads],
        pltpu.HBM((NPLANE, NZ, 32, LANES), bf16),
        unused=[in_hbm(relayed[0])],
    )
    heads = exchange(heads, PLANE)
    to_other = call(
        sums_kernel,
        [],
        [heads, other_lm],
        like((vocab, EXPERTS), f32),
        flops=2 * EXPERTS * D * vocab,
        moved=4 << 20,
        unused=[in_hbm(part) for part in sent],
    )
    to_own = call(
        sums_kernel,
        [],
        [heads, lm_head],
        like((vocab, EXPERTS), f32),
        flops=2 * EXPERTS * D * vocab,
        moved=4 << 20,
    )
    logits, stats = call(
        logits_kernel,
        [core_at],
        [to_own, swap(to_other)],
        [pltpu.HBM((2, vocab, EXPERTS), f32), pltpu.HBM((32, 4, EXPERTS), f32)],
        moved=1 << 20,
    )
    mixture = own
    for part in sent:
        mixture = mixture + part.astype(f32)
    layer_out = (hidden.astype(f32) + mixture).astype(bf16)
    stats = exchange(stats, ("x", "y", "c"))
    stats = call(merge_kernel, [], [stats], pltpu.HBM((NZ, 4, EXPERTS), f32))
    stats = exchange(stats, "z")
    logprob = finish(stats, logits)
    return (attended, layer_out, jnp.transpose(logprob, (0, 2, 1)))


def solution(mesh):
    fine = Mesh(mesh.devices.reshape(4, 8, 4, 2), ALL)
    in_specs = (
        P(EP, None, TP),
        P(None, EP, None, TP),
        P(None, EP, None, TP),
        P(EP),
        P(EP, None),
        P(EP, TP),
        P(),
        P(EP, None),
        P(EP, None),
        P(EP, None, TP),
        P(EP, None, TP),
        P(EP, TP, None),
        P(EP),
        P(),
        P(None, ALL, None),
        P(None, ALL),
        P(ALL, None),
    )
    out_specs = (P(EP, None, TP), P(EP, TP), P(None, None, ALL))
    return jax.shard_map(
        on_device, mesh=fine, in_specs=in_specs, out_specs=out_specs, check_vma=False
    )
```
